256 devices in a mesh: firm: 32 (over x_lo, z, core), day: 8 (over x_hi, y).
Axes of the slice: x: 4 (x_hi: 2, x_lo: 2; x = x_hi * 2 + x_lo), y: 4, z: 8, core: 2. Of those that a mesh axis runs over, the one named last changes fastest.
Arguments:
- residuals: float32 [32768, 16384], P('firm', 'day'), may hold values from -6 to 6
- loadings: float32 [32768, 8], P('firm'), may hold values from -6 to 6
- factor_path: float32 [16384, 8], P('day'), may hold values from -0.18 to 0.18
- start_guess: float32 [16384, 8], P('day'), may hold values from -6 to 6
- cluster_ids: int32 [32768], P('firm'), may hold values from 0 to 511
- sign_bits: int32 [512, 16], replicated, may hold values from 0 to 1
Outputs:
- boot_loadings: float32 [32768, 128], P('firm')
- boot_factors: float32 [16384, 128], P('day')
The draws below stay inside these ranges and needn't reach their ends.
All inputs are finite; a program needn't handle non-finite values.
Results may differ from the reference program's by a relative error of at most 0.0011.
Values sent between devices are 32-bit elements; how exact they have to be, the bound alone decides.
No kernel may reach another device: no remote copies, remote signals or barrier semaphores. Data moves between devices by JAX's collectives and lax.ppermute only.
A program may use at most 64 MiB of HBM per device.

```python
import jax
import jax.numpy as jnp
from jax import lax

FACTORS = 8
REPS = 16
CLUSTERS = 512
ITERS = 2
FIRMS = 32768
DAYS = 16384


def with_ends(values, stream_key, least, high):
    dims = values.shape
    index_at = [jax.random.randint(jax.random.fold_in(stream_key, axis), (), 0, dims[axis]) for axis in range(len(dims))]
    values = values.at[tuple(index_at)].set(least)
    longest = dims.index(max(dims))
    index_at[longest] = (index_at[longest] + 1) % dims[longest]
    return values.at[tuple(index_at)].set(high)


def level_of(key, extent, split, least, high):
    level = 1.0
    for dim, blocks in split:
        draws = jax.random.uniform(jax.random.fold_in(jax.random.fold_in(key, 6), dim), (blocks,), jnp.float32, least / len(split), high / len(split))
        level = level * jnp.repeat(jnp.exp(draws), extent[dim] // blocks).reshape((-1,) + (1,) * (len(extent) - 1 - dim))
    return level


def scatter_about(own_key, dims, spread, reach, pieces=(), held_as=jnp.bfloat16):
    entries = spread * jax.random.normal(own_key, dims, jnp.float32)
    if pieces:
        entries = entries * level_of(own_key, dims, pieces, -0.22, 0.18)
    return jnp.clip(entries, -reach, reach).astype(held_as)


def setup_inputs(seed: int = 0) -> dict:
    arg_keys = jax.random.split(jax.random.key(seed), 7)
    return {
        "residuals": scatter_about(arg_keys[0], (FIRMS, DAYS), 1.0, 6.0, ((0, 32), (1, 8)), jnp.float32),
        "loadings": scatter_about(arg_keys[1], (FIRMS, FACTORS), 1.0, 6.0, ((0, 32),), jnp.float32),
        "factor_path": scatter_about(arg_keys[2], (DAYS, FACTORS), 0.03, 0.18, ((0, 8),), jnp.float32),
        "start_guess": scatter_about(arg_keys[3], (DAYS, FACTORS), 1.0, 6.0, ((0, 8),), jnp.float32),
        "cluster_ids": with_ends(jax.random.randint(arg_keys[4], (FIRMS,), 0, CLUSTERS), jax.random.fold_in(arg_keys[4], 1), 0, CLUSTERS - 1).astype(jnp.int32),
        "sign_bits": with_ends(jax.random.randint(arg_keys[5], (CLUSTERS, REPS), 0, 2), jax.random.fold_in(arg_keys[5], 1), 0, 1).astype(jnp.int32),
    }


def gram_of(matrix):
    blocks = matrix.reshape(matrix.shape[0], REPS, FACTORS)
    return jnp.einsum('nbr,nbs->brs', blocks, blocks, precision=lax.Precision.HIGHEST)

def orthonormal(matrix):
    lower = jnp.linalg.cholesky(gram_of(matrix))
    eye_blocks = jnp.broadcast_to(jnp.eye(FACTORS, dtype=matrix.dtype), lower.shape)
    inverse = lax.linalg.triangular_solve(lower, eye_blocks, left_side=True, lower=True)
    blocks = matrix.reshape(matrix.shape[0], REPS, FACTORS)
    return jnp.einsum('nbr,bsr->nbs', blocks, inverse, precision=lax.Precision.HIGHEST).reshape(matrix.shape)

def reference(residuals, loadings, factor_path, start_guess, cluster_ids, sign_bits):
    highest = lax.Precision.HIGHEST
    signs = 2.0 * sign_bits.astype(jnp.float32) - 1.0
    row_signs = signs[cluster_ids]
    weights_wide = jnp.repeat(row_signs, FACTORS, axis=1).astype(residuals.dtype)
    current = jnp.tile(start_guess, (1, REPS))
    loads = None
    for sweep in range(ITERS):
        raw_loads = weights_wide * jnp.dot(residuals, current, precision=highest) + jnp.dot(loadings, jnp.dot(factor_path.T, current, precision=highest), precision=highest)
        loads = orthonormal(raw_loads)
        raw_factors = jnp.dot(residuals.T, weights_wide * loads, precision=highest) + jnp.dot(factor_path, jnp.dot(loadings.T, loads, precision=highest), precision=highest)
        current = orthonormal(raw_factors)
    return (jnp.sqrt(1.0 * FIRMS) * loads, jnp.sqrt(1.0 * DAYS) * current)
```

```python
import functools
import math

import jax
import jax.numpy as jnp
from jax import lax
from jax.experimental import pallas as pl
from jax.experimental.pallas import tpu as pltpu
from jax.sharding import Mesh
from jax.sharding import PartitionSpec as P

STEPS = 4
HIGHEST = lax.Precision.HIGHEST
NN = (((1,), (0,)), ((), ()))
NT = (((1,), (1,)), ((), ()))
TN = (((0,), (0,)), ((), ()))
PARAMS = pltpu.CompilerParams(vmem_limit_bytes=48 * 1024 * 1024)


def exact(a, b, dims):
    return lax.dot_general(a, b, dims, precision=HIGHEST, preferred_element_type=jnp.float32)


def fast(a, b, dims):
    return lax.dot_general(a, b, dims, preferred_element_type=jnp.float32)


def split(x):
    high = x.astype(jnp.bfloat16)
    return high, (x - high.astype(jnp.float32)).astype(jnp.bfloat16)


def compact(full, factors):
    n = full.shape[0]
    row = lax.broadcasted_iota(jnp.int32, (n, n), 0) // factors
    lane = lax.broadcasted_iota(jnp.int32, (n, n), 1) // factors
    kept = jnp.where(row == lane, full, 0.0)
    return kept.reshape(n // factors, factors, n).sum(axis=0)


def inverse_blocks(gram, factors):
    n = gram.shape[1]
    row = lax.broadcasted_iota(jnp.int32, (factors, n), 0)
    lane = lax.broadcasted_iota(jnp.int32, (factors, n), 1)
    first = (lane // factors) * factors
    rest = gram
    inverse = jnp.where(row == lane - first, 1.0, 0.0)
    for j in range(factors):
        column = jnp.take_along_axis(rest, first + j, axis=1, mode="promise_in_bounds")
        pivot = column[j : j + 1]
        ratio = jnp.where(row > j, column / pivot, 0.0)
        rest = rest - ratio * rest[j : j + 1]
        inverse = inverse - ratio * inverse[j : j + 1]
        inverse = jnp.where(row == j, inverse / jnp.sqrt(pivot), inverse)
    wide = jnp.concatenate([inverse] * (n // factors), axis=0)
    row = lax.broadcasted_iota(jnp.int32, (n, n), 0) // factors
    lane = lax.broadcasted_iota(jnp.int32, (n, n), 1) // factors
    return jnp.where(row == lane, wide, 0.0)


def signs_kernel(ids_ref, bits_ref, wide_ref, tall_ref, *, factors):
    reps, clusters = bits_ref.shape
    firms = ids_ref.shape[1]
    table = 2.0 * bits_ref[...].astype(jnp.float32) - 1.0
    table = jnp.broadcast_to(table[:, None, :], (reps, factors, clusters))
    table = table.reshape(reps * factors, clusters).astype(jnp.bfloat16)
    cluster = lax.broadcasted_iota(jnp.int32, (clusters, firms), 0)
    member = jnp.where(cluster == ids_ref[...], 1.0, 0.0).astype(jnp.bfloat16)
    wide = fast(table, member, NN)
    wide_ref[...] = wide
    tall_ref[...] = wide.T


def first_kernel(start_ref, factor_ref, res_ref, out_ref, start_split):
    step = pl.program_id(0)
    copies, factors, width = out_ref.shape
    rows = res_ref.shape[0]
    firms = rows * STEPS

    @pl.when(step == 0)
    def _():
        start = start_ref[...]
        high = start.astype(jnp.bfloat16).astype(jnp.float32)
        both = jnp.concatenate([high, start - high], axis=0).astype(jnp.bfloat16)
        start_split[...] = jnp.zeros_like(start_split)
        start_split[0 : 2 * factors, :] = both
        small = exact(start, factor_ref[...], NT)
        small = jnp.concatenate([small, jnp.zeros((factors, width - firms - factors), jnp.float32)], axis=1)
        out_ref[:, :, firms:] = jnp.broadcast_to(small[None], (copies, factors, width - firms))

    high, low = split(res_ref[...])
    part = fast(high, start_split[...], NT) + fast(low, start_split[...], NT)
    part = part.T
    part = part[0:factors] + part[factors : 2 * factors]
    out_ref[:, :, pl.ds(pl.multiple_of(step * rows, rows), rows)] = jnp.broadcast_to(part[None], (copies, factors, rows))


def days_from(raw_t, signs_ref, loadings_ref, left_ref, small_ref):
    factors = loadings_ref.shape[0]
    n = raw_t.shape[0]
    high, low = split(signs_ref[...] * raw_t)
    left_ref[0:n] = high
    left_ref[n:] = low
    small_ref[...] = exact(raw_t, loadings_ref[...], NT)
    return compact(exact(raw_t, raw_t, NT), factors)


def days_tile(step, factor_ref, res_ref, left_ref, small_ref, send_ref, keep_ref):
    n = small_ref.shape[0]
    rows = send_ref.shape[1] - factor_ref.shape[0]
    high, low = split(res_ref[...])
    both = fast(left_ref[...], high, NN)
    tile = both[0:n] + both[n:] + fast(left_ref[0:n], low, NN) + exact(small_ref[...], factor_ref[...], NN)
    tile = tile.T
    tile = tile.reshape(tile.shape[0] // rows, rows, n)
    half = STEPS // 2
    at = pl.ds(lax.rem(step, half) * tile.shape[0], tile.shape[0])

    @pl.when(step < half)
    def _():
        send_ref[at, 0:rows, :] = tile

    @pl.when(step >= half)
    def _():
        keep_ref[at, 0:rows, :] = tile


def put_gram(gram, send_ref, keep_ref):
    copies, rows, n = send_ref.shape
    wide = jnp.broadcast_to(gram[None], (copies, gram.shape[0], n))
    send_ref[:, rows - gram.shape[0] :, :] = wide
    keep_ref[:, rows - gram.shape[0] :, :] = wide


def days_first_kernel(core_ref, got_ref, signs_ref, loadings_ref, factor_ref, res_ref, send_ref, keep_ref, left_ref, small_ref):
    step = pl.program_id(0)

    @pl.when(step == 0)
    def _():
        factors, firms = loadings_ref.shape
        n = signs_ref.shape[0]
        got = got_ref[...].sum(axis=0)
        by_residuals, mixed = got[:, 0:firms], got[:, firms : firms + factors]
        by_factors = jnp.zeros((factors, firms), jnp.float32)
        for m in range(factors):
            by_factors = by_factors + mixed[:, m : m + 1] * loadings_ref[m : m + 1, :]
        copies = n // factors
        raw_t = signs_ref[...] * jnp.concatenate([by_residuals] * copies, axis=0)
        raw_t = raw_t + jnp.concatenate([by_factors] * copies, axis=0)
        put_gram(days_from(raw_t, signs_ref, loadings_ref, left_ref, small_ref), send_ref, keep_ref)

    days_tile(step, factor_ref, res_ref, left_ref, small_ref, send_ref, keep_ref)


def days_later_kernel(core_ref, got_ref, gram_ref, signs_ref, loadings_ref, factor_ref, res_ref, send_ref, keep_ref, raw_ref, left_ref, small_ref):
    step = pl.program_id(0)

    @pl.when(step == 0)
    def _():
        raw = exact(got_ref[...], inverse_blocks(gram_ref[...], loadings_ref.shape[0]), NT)
        raw_ref[...] = raw
        put_gram(days_from(raw.T, signs_ref, loadings_ref, left_ref, small_ref), send_ref, keep_ref)

    days_tile(step, factor_ref, res_ref, left_ref, small_ref, send_ref, keep_ref)


def firms_kernel(core_ref, mine_ref, other_ref, gram_ref, signs_ref, loadings_ref, factor_ref, res_ref, out_ref, raw_ref, right_ref, add_ref):
    step = pl.program_id(0)
    factors = loadings_ref.shape[0]
    half, n = mine_ref.shape
    rows = res_ref.shape[0]

    @pl.when(step == 0)
    def _():
        inverse = inverse_blocks(gram_ref[...], factors)
        core = core_ref[0]
        raw_ref[pl.ds(pl.multiple_of(core * half, half), half), :] = exact(mine_ref[...], inverse, NT)
        raw_ref[pl.ds(pl.multiple_of((1 - core) * half, half), half), :] = exact(other_ref[...], inverse, NT)
        raw = raw_ref[...]
        high, low = split(raw)
        right_ref[:, 0:n] = high
        right_ref[:, n:] = low
        gram = compact(exact(raw, raw, TN), factors)
        copies, total = out_ref.shape[0], out_ref.shape[1]
        out_ref[:, total - factors :, :] = jnp.broadcast_to(gram[None], (copies, factors, n))
        add_ref[...] = exact(loadings_ref[...], exact(factor_ref[...], raw, NN), TN)

    high, low = split(res_ref[...])
    both = fast(high, right_ref[...], NN)
    part = both[:, 0:n] + both[:, n:] + fast(low, right_ref[:, 0:n], NN)
    at = pl.ds(pl.multiple_of(step * rows, rows), rows)
    part = signs_ref[at, :] * part + add_ref[at, :]
    block = out_ref.shape[1] - factors
    part = part.reshape(rows // block, block, n)
    out_ref[pl.ds(step * (rows // block), rows // block), 0:block, :] = part


def last_kernel(core_ref, mine_ref, other_ref, gram_ref, raw_ref, out_ref, inverse_ref):
    factors = gram_ref.shape[0]
    half, n = mine_ref.shape
    inverse = inverse_blocks(gram_ref[...], factors)
    inverse_ref[...] = inverse
    core = core_ref[0]
    raw_ref[pl.ds(pl.multiple_of(core * half, half), half), :] = exact(mine_ref[...], inverse, NT)
    raw_ref[pl.ds(pl.multiple_of((1 - core) * half, half), half), :] = exact(other_ref[...], inverse, NT)
    raw = raw_ref[...]
    out_ref[...] = jnp.broadcast_to(compact(exact(raw, raw, TN), factors)[None], out_ref.shape)


def loadings_kernel(raw_ref, inverse_ref, out_ref, *, scale):
    out_ref[...] = scale * exact(raw_ref[...], inverse_ref[...], NT)


def factors_kernel(got_ref, raw_ref, out_ref, *, scale):
    gram = got_ref[...].sum(axis=0)
    out_ref[...] = scale * exact(raw_ref[...], inverse_blocks(gram, gram.shape[0]), NT)


def shape(*dims):
    return jax.ShapeDtypeStruct(dims, jnp.float32)


def whole(*dims):
    return pl.BlockSpec(dims, lambda *_: (0,) * len(dims))


def on_device(residuals, loadings, factor_path, start_guess, cluster_ids, sign_bits, *, chips, total_firms, total_days, day_ranks):
    firms, days = residuals.shape
    factors = start_guess.shape[1]
    clusters, reps = sign_bits.shape
    n = reps * factors
    half = days // 2
    chunk = half // chips
    block = firms // day_ranks
    loadings_t, factor_t, start_t = loadings.T, factor_path.T, start_guess.T
    core = lax.axis_index("core").astype(jnp.int32).reshape(1)

    signs_t, signs = pl.pallas_call(
        functools.partial(signs_kernel, factors=factors),
        out_shape=(shape(n, firms), shape(firms, n)),
        compiler_params=PARAMS,
        name="signs",
    )(cluster_ids.reshape(1, firms), sign_bits.T)

    first = pl.pallas_call(
        first_kernel,
        grid=(STEPS,),
        in_specs=[whole(factors, days), whole(factors, days), pl.BlockSpec((firms // STEPS, days), lambda t: (t, 0))],
        out_specs=whole(day_ranks, factors, firms + n),
        out_shape=shape(day_ranks, factors, firms + n),
        scratch_shapes=[pltpu.VMEM((n, days), jnp.bfloat16)],
        compiler_params=PARAMS,
        name="first",
    )(start_t, factor_t, residuals)
    first = lax.all_to_all(first, ("x_hi", "y"), 0, 0, tiled=True)

    tiles = STEPS // 2

    def tile_of(t, core_ref):
        side = jnp.where(t < tiles, 1 - core_ref[0], core_ref[0])
        return side * tiles + lax.rem(t, tiles)

    day_specs = [
        pl.BlockSpec((factors, days // STEPS), lambda t, c: (0, tile_of(t, c))),
        pl.BlockSpec((firms, days // STEPS), lambda t, c: (0, tile_of(t, c))),
    ]
    day_scratch = [pltpu.VMEM((2 * n, firms), jnp.bfloat16), pltpu.VMEM((n, factors), jnp.float32)]
    parts = (chips, chunk + factors, n)

    def sum_firms(send, keep):
        pair = keep + lax.ppermute(send, "core", [(0, 1), (1, 0)])
        got = lax.all_to_all(pair, ("x_lo", "z"), 0, 0, tiled=True).sum(axis=0)
        mine = jnp.broadcast_to(got[None, 0:chunk], (chips, chunk, n))
        mine = lax.all_to_all(mine, ("x_lo", "z"), 0, 0, tiled=True).reshape(half, n)
        return mine, lax.ppermute(mine, "core", [(0, 1), (1, 0)]), got[chunk:]

    send, keep = pl.pallas_call(
        days_first_kernel,
        grid_spec=pltpu.PrefetchScalarGridSpec(
            num_scalar_prefetch=1,
            grid=(STEPS,),
            in_specs=[whole(day_ranks, factors, firms + n), whole(n, firms), whole(factors, firms), *day_specs],
            out_specs=[whole(*parts), whole(*parts)],
            scratch_shapes=day_scratch,
        ),
        out_shape=(shape(*parts), shape(*parts)),
        compiler_params=PARAMS,
        name="days_first",
    )(core, first, signs_t, loadings_t, factor_t, residuals)
    mine, other, gram = sum_firms(send, keep)

    by_day = pl.pallas_call(
        firms_kernel,
        grid_spec=pltpu.PrefetchScalarGridSpec(
            num_scalar_prefetch=1,
            grid=(STEPS,),
            in_specs=[
                whole(half, n),
                whole(half, n),
                whole(factors, n),
                whole(firms, n),
                whole(factors, firms),
                whole(factors, days),
                pl.BlockSpec((firms // STEPS, days), lambda t, c: (t, 0)),
            ],
            out_specs=whole(day_ranks, block + factors, n),
            scratch_shapes=[
                pltpu.VMEM((days, n), jnp.float32),
                pltpu.VMEM((days, 2 * n), jnp.bfloat16),
                pltpu.VMEM((firms, n), jnp.float32),
            ],
        ),
        out_shape=shape(day_ranks, block + factors, n),
        compiler_params=PARAMS,
        name="firms",
    )(core, mine, other, gram, signs, loadings_t, factor_t, residuals)
    got = lax.all_to_all(by_day, ("x_hi", "y"), 0, 0, tiled=True).sum(axis=0)
    gram = got[block:]
    wide = jnp.broadcast_to(got[None, 0:block], (day_ranks, block, n))
    wide = lax.all_to_all(wide, ("x_hi", "y"), 0, 0, tiled=True).reshape(firms, n)

    send, keep, raw_loads = pl.pallas_call(
        days_later_kernel,
        grid_spec=pltpu.PrefetchScalarGridSpec(
            num_scalar_prefetch=1,
            grid=(STEPS,),
            in_specs=[whole(firms, n), whole(factors, n), whole(n, firms), whole(factors, firms), *day_specs],
            out_specs=[whole(*parts), whole(*parts), whole(firms, n)],
            scratch_shapes=day_scratch,
        ),
        out_shape=(shape(*parts), shape(*parts), shape(firms, n)),
        compiler_params=PARAMS,
        name="days_later",
    )(core, wide, gram, signs_t, loadings_t, factor_t, residuals)
    mine, other, gram = sum_firms(send, keep)

    raw_factors, last, inverse = pl.pallas_call(
        last_kernel,
        in_specs=[pl.BlockSpec(memory_space=pltpu.SMEM)] + [pl.BlockSpec(memory_space=pltpu.VMEM)] * 3,
        out_shape=(shape(days, n), shape(day_ranks, factors, n), shape(n, n)),
        compiler_params=PARAMS,
        name="last",
    )(core, mine, other, gram)
    last = lax.all_to_all(last, ("x_hi", "y"), 0, 0, tiled=True)
    boot_loadings = pl.pallas_call(
        functools.partial(loadings_kernel, scale=math.sqrt(total_firms)),
        out_shape=shape(firms, n),
        compiler_params=PARAMS,
        name="boot_loadings",
    )(raw_loads, inverse)
    boot_factors = pl.pallas_call(
        functools.partial(factors_kernel, scale=math.sqrt(total_days)),
        out_shape=shape(days, n),
        compiler_params=PARAMS,
        name="boot_factors",
    )(last, raw_factors)
    return boot_loadings, boot_factors


def solution(mesh):
    firm_ranks, day_ranks = mesh.shape["firm"], mesh.shape["day"]
    axes = ("x_lo", "z", "core", "x_hi", "y")
    fine = Mesh(mesh.devices.reshape(2, firm_ranks // 4, 2, 2, day_ranks // 2), axes)
    firm, day = ("x_lo", "z", "core"), ("x_hi", "y")

    def run(residuals, *rest):
        total_firms, total_days = residuals.shape
        body = functools.partial(
            on_device, chips=firm_ranks // 2, total_firms=total_firms, total_days=total_days, day_ranks=day_ranks
        )
        return jax.shard_map(
            body,
            mesh=fine,
            in_specs=(P(firm, day), P(firm, None), P(day, None), P(day, None), P(firm), P()),
            out_specs=(P(firm, None), P(day, None)),
            check_vma=False,
        )(residuals, *rest)

    return run
```

```python
import functools
import math

import jax
import jax.numpy as jnp
from jax import lax
from jax.experimental import pallas as pl
from jax.experimental.pallas import tpu as pltpu
from jax.sharding import Mesh
from jax.sharding import PartitionSpec as P

STEPS = 4
AHEAD = 4
HIGHEST = lax.Precision.HIGHEST
NN = (((1,), (0,)), ((), ()))
NT = (((1,), (1,)), ((), ()))
TN = (((0,), (0,)), ((), ()))
PARAMS = pltpu.CompilerParams(vmem_limit_bytes=32 * 1024 * 1024)


def exact(a, b, dims):
    return lax.dot_general(a, b, dims, precision=HIGHEST, preferred_element_type=jnp.float32)


def fast(a, b, dims):
    return lax.dot_general(a, b, dims, preferred_element_type=jnp.float32)


def split(x):
    high = x.astype(jnp.bfloat16)
    return high, (x - high.astype(jnp.float32)).astype(jnp.bfloat16)


def compact(full, factors):
    n = full.shape[0]
    row = lax.broadcasted_iota(jnp.int32, (n, n), 0) // factors
    lane = lax.broadcasted_iota(jnp.int32, (n, n), 1) // factors
    kept = jnp.where(row == lane, full, 0.0)
    return kept.reshape(n // factors, factors, n).sum(axis=0)


def inverse_blocks(gram, factors):
    n = gram.shape[1]
    row = lax.broadcasted_iota(jnp.int32, (factors, n), 0)
    lane = lax.broadcasted_iota(jnp.int32, (factors, n), 1)
    first = (lane // factors) * factors
    rest = gram
    inverse = jnp.where(row == lane - first, 1.0, 0.0)
    for j in range(factors):
        column = jnp.take_along_axis(rest, first + j, axis=1, mode="promise_in_bounds")
        pivot = column[j : j + 1]
        ratio = jnp.where(row > j, column / pivot, 0.0)
        rest = rest - ratio * rest[j : j + 1]
        inverse = inverse - ratio * inverse[j : j + 1]
        inverse = jnp.where(row == j, inverse / jnp.sqrt(pivot), inverse)
    wide = jnp.concatenate([inverse] * (n // factors), axis=0)
    row = lax.broadcasted_iota(jnp.int32, (n, n), 0) // factors
    lane = lax.broadcasted_iota(jnp.int32, (n, n), 1) // factors
    return jnp.where(row == lane, wide, 0.0)


def put_signs(ids_ref, bits_ref, wide_ref, tall_ref):
    reps, clusters = bits_ref.shape
    n, firms = wide_ref.shape
    table = 2.0 * bits_ref[...].astype(jnp.float32) - 1.0
    table = jnp.broadcast_to(table[:, None, :], (reps, n // reps, clusters))
    table = table.reshape(n, clusters).astype(jnp.bfloat16)
    cluster = lax.broadcasted_iota(jnp.int32, (clusters, firms), 0)
    member = jnp.where(cluster == ids_ref[...], 1.0, 0.0).astype(jnp.bfloat16)
    wide = fast(table, member, NN)
    wide_ref[...] = wide
    tall_ref[...] = wide.T


def columns(t, width):
    return (slice(None), slice(t * width, (t + 1) * width))


def rows_of(t, rows):
    return (slice(t * rows, (t + 1) * rows), slice(None))


def bring(res_any, res_ref, sems, tiles):
    copies = [pltpu.make_async_copy(res_any.at[tile], res_ref.at[tile], sems.at[t]) for t, tile in enumerate(tiles)]
    for copy in copies[:AHEAD]:
        copy.start()
    return copies


def arrive(copies, t):
    copies[t].wait()
    if t + AHEAD < len(copies):
        copies[t + AHEAD].start()


def first_kernel(
    start_any, factor_any, ids_any, bits_any, res_any,
    out_ref, wide_ref, tall_ref,
    start_ref, factor_ref, ids_ref, bits_ref, res_ref, total_ref, sems,
):
    copies, factors, width = out_ref.shape
    firms, days = res_ref.shape
    n = total_ref.shape[1]
    pairs = [(start_any, start_ref), (factor_any, factor_ref), (ids_any, ids_ref), (bits_any, bits_ref)]
    small = [pltpu.make_async_copy(a, b, sems.at[STEPS + i]) for i, (a, b) in enumerate(pairs)]
    for copy in small:
        copy.start()
    tiles = [columns(t, days // STEPS) for t in range(STEPS)]
    large = bring(res_any, res_ref, sems, tiles)
    for copy in small:
        copy.wait()
    start = start_ref[...]
    high = start.astype(jnp.bfloat16).astype(jnp.float32)
    both = jnp.concatenate([high, start - high, jnp.zeros((n - 2 * factors, days), jnp.float32)], axis=0)
    both = both.T.astype(jnp.bfloat16)
    mixed = exact(start, factor_ref[...], NT)
    mixed = jnp.concatenate([mixed, jnp.zeros((factors, width - firms - factors), jnp.float32)], axis=1)
    out_ref[:, :, firms:] = jnp.broadcast_to(mixed[None], (copies, factors, width - firms))
    put_signs(ids_ref, bits_ref, wide_ref, tall_ref)
    for t in range(STEPS):
        arrive(large, t)
        high, low = split(res_ref[tiles[t]])
        right = both[t * (days // STEPS) : (t + 1) * (days // STEPS)]
        part = fast(high, right, NN) + fast(low, right, NN)
        total_ref[...] = part if t == 0 else total_ref[...] + part
    total = total_ref[...].T
    total = total[0:factors] + total[factors : 2 * factors]
    out_ref[:, :, 0:firms] = jnp.broadcast_to(total[None], (copies, factors, firms))


def days_from(raw_t, signs_ref, loadings_ref, left_ref, small_ref):
    factors = loadings_ref.shape[0]
    n = raw_t.shape[0]
    high, low = split(signs_ref[...] * raw_t)
    left_ref[0:n] = high
    left_ref[n:] = low
    small_ref[...] = exact(raw_t, loadings_ref[...], NT)
    return compact(exact(raw_t, raw_t, NT), factors)


def days_tiles(core, copies, tiles, factor_ref, res_ref, left_ref, small_ref, send_ref, keep_ref):
    n = small_ref.shape[0]
    rows = send_ref.shape[1] - factor_ref.shape[0]
    width = res_ref.shape[1] // STEPS
    half = STEPS // 2
    for t in range(STEPS):
        arrive(copies, t)
        high, low = split(res_ref[tiles[t]])
        both = fast(left_ref[...], high, NN)
        tile = both[0:n] + both[n:] + fast(left_ref[0:n], low, NN) + exact(small_ref[...], factor_ref[tiles[t]], NN)
        tile = tile.T.reshape(width // rows, rows, n)
        at = slice(t % half * (width // rows), (t % half + 1) * (width // rows))

        @pl.when(core != t // half)
        def _():
            send_ref[at, 0:rows, :] = tile

        @pl.when(core == t // half)
        def _():
            keep_ref[at, 0:rows, :] = tile


def put_gram(gram, send_ref, keep_ref):
    copies, rows, n = send_ref.shape
    wide = jnp.broadcast_to(gram[None], (copies, gram.shape[0], n))
    send_ref[:, rows - gram.shape[0] :, :] = wide
    keep_ref[:, rows - gram.shape[0] :, :] = wide


def days_first_kernel(core_ref, got_ref, signs_ref, loadings_ref, factor_ref, res_any, send_ref, keep_ref, left_ref, small_ref, res_ref, sems):
    tiles = [columns(t, res_ref.shape[1] // STEPS) for t in range(STEPS)]
    copies = bring(res_any, res_ref, sems, tiles)
    factors, firms = loadings_ref.shape
    n = signs_ref.shape[0]
    got = got_ref[...].sum(axis=0)
    by_residuals, mixed = got[:, 0:firms], got[:, firms : firms + factors]
    by_factors = jnp.zeros((factors, firms), jnp.float32)
    for m in range(factors):
        by_factors = by_factors + mixed[:, m : m + 1] * loadings_ref[m : m + 1, :]
    reps = n // factors
    raw_t = signs_ref[...] * jnp.concatenate([by_residuals] * reps, axis=0)
    raw_t = raw_t + jnp.concatenate([by_factors] * reps, axis=0)
    put_gram(days_from(raw_t, signs_ref, loadings_ref, left_ref, small_ref), send_ref, keep_ref)
    days_tiles(core_ref[0], copies, tiles, factor_ref, res_ref, left_ref, small_ref, send_ref, keep_ref)


def days_later_kernel(core_ref, got_ref, signs_ref, loadings_ref, factor_ref, res_any, send_ref, keep_ref, left_ref, small_ref, res_ref, sems):
    tiles = [columns(t, res_ref.shape[1] // STEPS) for t in range(STEPS)]
    copies = bring(res_any, res_ref, sems, tiles)
    put_gram(days_from(got_ref[...].T, signs_ref, loadings_ref, left_ref, small_ref), send_ref, keep_ref)
    days_tiles(core_ref[0], copies, tiles, factor_ref, res_ref, left_ref, small_ref, send_ref, keep_ref)


def firms_kernel(core_ref, mine_ref, other_ref, signs_ref, loadings_ref, factor_ref, res_any, out_ref, raw_ref, right_ref, add_ref, res_ref, sems):
    factors = loadings_ref.shape[0]
    half, n = mine_ref.shape
    rows = res_ref.shape[0] // STEPS
    tiles = [rows_of(t, rows) for t in range(STEPS)]
    large = bring(res_any, res_ref, sems, tiles)
    core = core_ref[0]
    raw_ref[pl.ds(pl.multiple_of(core * half, half), half), :] = mine_ref[...]
    raw_ref[pl.ds(pl.multiple_of((1 - core) * half, half), half), :] = other_ref[...]
    raw = raw_ref[...]
    high, low = split(raw)
    right_ref[:, 0:n] = high
    right_ref[:, n:] = low
    gram = compact(exact(raw, raw, TN), factors)
    copies, total = out_ref.shape[0], out_ref.shape[1]
    out_ref[:, total - factors :, :] = jnp.broadcast_to(gram[None], (copies, factors, n))
    add_ref[...] = exact(loadings_ref[...], exact(factor_ref[...], raw, NN), TN)
    block = total - factors
    for t in range(STEPS):
        arrive(large, t)
        at = slice(t * rows, (t + 1) * rows)
        high, low = split(res_ref[at, :])
        both = fast(high, right_ref[...], NN)
        part = both[:, 0:n] + both[:, n:] + fast(low, right_ref[:, 0:n], NN)
        part = signs_ref[at, :] * part + add_ref[at, :]
        out_ref[t * rows // block : (t + 1) * rows // block, 0:block, :] = part.reshape(rows // block, block, n)


def turn_kernel(got_ref, out_ref, inverse_ref):
    copies, rows, _ = out_ref.shape
    total = got_ref[...].sum(axis=0)
    inverse = inverse_blocks(total[rows:], total.shape[0] - rows)
    inverse_ref[...] = inverse
    chunk = exact(total[0:rows], inverse, NT)
    out_ref[...] = jnp.broadcast_to(chunk[None], out_ref.shape)


def last_kernel(core_ref, mine_ref, other_ref, raw_ref, out_ref):
    half = mine_ref.shape[0]
    mine, other = mine_ref[...], other_ref[...]
    core = core_ref[0]
    raw_ref[pl.ds(pl.multiple_of(core * half, half), half), :] = mine
    raw_ref[pl.ds(pl.multiple_of((1 - core) * half, half), half), :] = other
    gram = compact(exact(mine, mine, TN) + exact(other, other, TN), out_ref.shape[1])
    out_ref[...] = jnp.broadcast_to(gram[None], out_ref.shape)


def loadings_kernel(raw_ref, inverse_ref, out_ref, *, scale):
    out_ref[...] = scale * exact(raw_ref[...], inverse_ref[...], NT)


def factors_kernel(got_ref, raw_ref, out_ref, *, scale):
    gram = got_ref[...].sum(axis=0)
    out_ref[...] = scale * exact(raw_ref[...], inverse_blocks(gram, gram.shape[0]), NT)


def shape(*dims):
    return jax.ShapeDtypeStruct(dims, jnp.float32)


def inputs(count):
    small = [pl.BlockSpec(memory_space=pltpu.VMEM)] * count
    return [pl.BlockSpec(memory_space=pltpu.SMEM), *small]


def in_hbm(x):
    return pltpu.with_memory_space_constraint(x, pltpu.HBM)


def on_device(residuals, loadings, factor_path, start_guess, cluster_ids, sign_bits, *, chips, total_firms, total_days, day_ranks):
    firms, days = residuals.shape
    factors = start_guess.shape[1]
    clusters, reps = sign_bits.shape
    n = reps * factors
    half = days // 2
    chunk = half // chips
    block = firms // day_ranks
    loadings_t, factor_t, start_t = loadings.T, factor_path.T, start_guess.T
    core = lax.axis_index("core").astype(jnp.int32).reshape(1)

    residuals = in_hbm(residuals)
    block_scratch = [pltpu.VMEM((firms, days), jnp.float32), pltpu.SemaphoreType.DMA((STEPS,))]
    first, signs_t, signs = pl.pallas_call(
        first_kernel,
        in_specs=[pl.BlockSpec(memory_space=pl.ANY)] * 5,
        out_shape=(
            shape(day_ranks, factors, firms + n),
            shape(n, firms),
            shape(firms, n),
        ),
        scratch_shapes=[
            pltpu.VMEM((factors, days), jnp.float32),
            pltpu.VMEM((factors, days), jnp.float32),
            pltpu.VMEM((1, firms), jnp.int32),
            pltpu.VMEM((reps, clusters), jnp.int32),
            pltpu.VMEM((firms, days), jnp.float32),
            pltpu.VMEM((firms, n), jnp.float32),
            pltpu.SemaphoreType.DMA((STEPS + 4,)),
        ],
        compiler_params=PARAMS,
        name="first",
    )(in_hbm(start_t), in_hbm(factor_t), in_hbm(cluster_ids.reshape(1, firms)), in_hbm(sign_bits.T), residuals)
    first = lax.all_to_all(first, ("x_hi", "y"), 0, 0, tiled=True)

    day_scratch = [pltpu.VMEM((2 * n, firms), jnp.bfloat16), pltpu.VMEM((n, factors), jnp.float32), *block_scratch]
    parts = (chips, chunk + factors, n)

    def turn(got, rows):
        return pl.pallas_call(
            turn_kernel,
            out_shape=(shape(got.shape[0], rows, n), shape(n, n)),
            compiler_params=PARAMS,
            name="turn",
        )(got)

    def sum_firms(send, keep):
        pair = keep + lax.ppermute(send, "core", [(0, 1), (1, 0)])
        mine, inverse = turn(lax.all_to_all(pair, ("x_lo", "z"), 0, 0, tiled=True), chunk)
        mine = lax.all_to_all(mine, ("x_lo", "z"), 0, 0, tiled=True).reshape(half, n)
        return mine, lax.ppermute(mine, "core", [(0, 1), (1, 0)]), inverse

    send, keep = pl.pallas_call(
        days_first_kernel,
        in_specs=inputs(4) + [pl.BlockSpec(memory_space=pl.ANY)],
        scratch_shapes=day_scratch,
        out_shape=(shape(*parts), shape(*parts)),
        compiler_params=PARAMS,
        name="days_first",
    )(core, first, signs_t, loadings_t, factor_t, residuals)
    mine, other, _ = sum_firms(send, keep)

    by_day = pl.pallas_call(
        firms_kernel,
        in_specs=inputs(5) + [pl.BlockSpec(memory_space=pl.ANY)],
        scratch_shapes=[
            pltpu.VMEM((days, n), jnp.float32),
            pltpu.VMEM((days, 2 * n), jnp.bfloat16),
            pltpu.VMEM((firms, n), jnp.float32),
            *block_scratch,
        ],
        out_shape=shape(day_ranks, block + factors, n),
        compiler_params=PARAMS,
        name="firms",
    )(core, mine, other, signs, loadings_t, factor_t, residuals)
    raw_loads, _ = turn(lax.all_to_all(by_day, ("x_hi", "y"), 0, 0, tiled=True), block)
    raw_loads = lax.all_to_all(raw_loads, ("x_hi", "y"), 0, 0, tiled=True).reshape(firms, n)

    send, keep = pl.pallas_call(
        days_later_kernel,
        in_specs=inputs(4) + [pl.BlockSpec(memory_space=pl.ANY)],
        scratch_shapes=day_scratch,
        out_shape=(shape(*parts), shape(*parts)),
        compiler_params=PARAMS,
        name="days_later",
    )(core, raw_loads, signs_t, loadings_t, factor_t, residuals)
    mine, other, inverse = sum_firms(send, keep)

    raw_factors, last = pl.pallas_call(
        last_kernel,
        in_specs=inputs(2),
        out_shape=(shape(days, n), shape(day_ranks, factors, n)),
        compiler_params=PARAMS,
        name="last",
    )(core, mine, other)
    last = lax.all_to_all(last, ("x_hi", "y"), 0, 0, tiled=True)
    boot_loadings = pl.pallas_call(
        functools.partial(loadings_kernel, scale=math.sqrt(total_firms)),
        out_shape=shape(firms, n),
        compiler_params=PARAMS,
        name="boot_loadings",
    )(raw_loads, inverse)
    boot_factors = pl.pallas_call(
        functools.partial(factors_kernel, scale=math.sqrt(total_days)),
        out_shape=shape(days, n),
        compiler_params=PARAMS,
        name="boot_factors",
    )(last, raw_factors)
    return boot_loadings, boot_factors


def solution(mesh):
    firm_ranks, day_ranks = mesh.shape["firm"], mesh.shape["day"]
    axes = ("x_lo", "z", "core", "x_hi", "y")
    fine = Mesh(mesh.devices.reshape(2, firm_ranks // 4, 2, 2, day_ranks // 2), axes)
    firm, day = ("x_lo", "z", "core"), ("x_hi", "y")

    def run(residuals, *rest):
        total_firms, total_days = residuals.shape
        body = functools.partial(
            on_device, chips=firm_ranks // 2, total_firms=total_firms, total_days=total_days, day_ranks=day_ranks
        )
        return jax.shard_map(
            body,
            mesh=fine,
            in_specs=(P(firm, day), P(firm, None), P(day, None), P(day, None), P(firm), P()),
            out_specs=(P(firm, None), P(day, None)),
            check_vma=False,
        )(residuals, *rest)

    return run
```

```python
import functools
import math

import jax
import jax.numpy as jnp
from jax import lax
from jax.experimental import pallas as pl
from jax.experimental.pallas import tpu as pltpu
from jax.sharding import Mesh
from jax.sharding import PartitionSpec as P

STEPS = 4
PIECES = 2
AHEAD = 8
HIGHEST = lax.Precision.HIGHEST
NN = (((1,), (0,)), ((), ()))
NT = (((1,), (1,)), ((), ()))
TN = (((0,), (0,)), ((), ()))
PARAMS = pltpu.CompilerParams(vmem_limit_bytes=32 * 1024 * 1024)


def exact(a, b, dims):
    return lax.dot_general(a, b, dims, precision=HIGHEST, preferred_element_type=jnp.float32)


def fast(a, b, dims):
    return lax.dot_general(a, b, dims, preferred_element_type=jnp.float32)


def split(x):
    high = x.astype(jnp.bfloat16)
    return high, (x - high.astype(jnp.float32)).astype(jnp.bfloat16)


def split3(x):
    high = x.astype(jnp.bfloat16)
    rest = x - high.astype(jnp.float32)
    middle = rest.astype(jnp.bfloat16)
    return high, middle, (rest - middle.astype(jnp.float32)).astype(jnp.bfloat16)


def corners(both, rows, cols):
    return both[:rows, :cols] + (both[:rows, cols:] + both[rows:, :cols] + both[rows:, cols:])


def gram_of(high, middle, low, dims, axis):
    both = jnp.concatenate([high, middle], axis=axis)
    n = both.shape[axis] // 2
    cross = fast(high, low, dims)
    return corners(fast(both, both, dims), n, n) + (cross + cross.T)


def stack(x, order):
    high = x.astype(jnp.bfloat16).astype(jnp.float32)
    parts = {"h": high, "l": x - high, "0": jnp.zeros_like(x)}
    return jnp.concatenate([parts[p] for p in order], axis=0).astype(jnp.bfloat16)


def rotated(x, inverse):
    n = inverse.shape[0]
    high, low = split(x)
    top, rest = split(inverse.T)
    right = jnp.concatenate(
        [jnp.concatenate([top, rest], axis=1), jnp.concatenate([top, jnp.zeros_like(rest)], axis=1)], axis=0
    )
    both = fast(jnp.concatenate([high, low], axis=1), right, NN)
    return both[:, 0:n] + both[:, n:]


def compact(full, factors):
    n = full.shape[0]
    row = lax.broadcasted_iota(jnp.int32, (n, n), 0) // factors
    lane = lax.broadcasted_iota(jnp.int32, (n, n), 1) // factors
    kept = jnp.where(row == lane, full, 0.0)
    return kept.reshape(n // factors, factors, n).sum(axis=0)


def inverse_blocks(gram, factors):
    n = gram.shape[1]
    row = lax.broadcasted_iota(jnp.int32, (factors, n), 0)
    lane = lax.broadcasted_iota(jnp.int32, (factors, n), 1)
    first = (lane // factors) * factors
    rest = gram
    inverse = jnp.where(row == lane - first, 1.0, 0.0)
    for j in range(factors):
        column = jnp.take_along_axis(rest, first + j, axis=1, mode="promise_in_bounds")
        pivot = column[j : j + 1]
        ratio = jnp.where(row > j, column / pivot, 0.0)
        rest = rest - ratio * rest[j : j + 1]
        inverse = inverse - ratio * inverse[j : j + 1]
        inverse = jnp.where(row == j, inverse / jnp.sqrt(pivot), inverse)
    wide = jnp.concatenate([inverse] * (n // factors), axis=0)
    row = lax.broadcasted_iota(jnp.int32, (n, n), 0) // factors
    lane = lax.broadcasted_iota(jnp.int32, (n, n), 1) // factors
    return jnp.where(row == lane, wide, 0.0)


def put_signs(ids_ref, bits_ref, wide_ref, tall_ref):
    reps, clusters = bits_ref.shape
    n, firms = wide_ref.shape
    table = 2.0 * bits_ref[...].astype(jnp.float32) - 1.0
    table = jnp.broadcast_to(table[:, None, :], (reps, n // reps, clusters))
    table = table.reshape(n, clusters).astype(jnp.bfloat16)
    cluster = lax.broadcasted_iota(jnp.int32, (clusters, firms), 0)
    member = jnp.where(cluster == ids_ref[...], 1.0, 0.0).astype(jnp.bfloat16)
    wide = fast(table, member, NN)
    wide_ref[...] = wide
    tall_ref[...] = wide.T


def columns(t, width):
    return (slice(None), slice(t * width, (t + 1) * width))


def rows_of(t, rows):
    return (slice(t * rows, (t + 1) * rows), slice(None))


def bring(pairs, sems):
    copies = [pltpu.make_async_copy(a, b, sems.at[t]) for t, (a, b) in enumerate(pairs)]
    for copy in copies[:AHEAD]:
        copy.start()
    return copies


def arrive(copies, t):
    for p in range(t * PIECES, (t + 1) * PIECES):
        copies[p].wait()
        if p + AHEAD < len(copies):
            copies[p + AHEAD].start()


def piece_pairs(res_any, res_ref, piece):
    size = res_ref.shape[1] if piece is columns else res_ref.shape[0]
    count = STEPS * PIECES
    return [(res_any.at[piece(p, size // count)], res_ref.at[piece(p, size // count)]) for p in range(count)]


def bring_for_core(core, res_any, res_ref, sems):
    days = res_ref.shape[1]
    count = STEPS * PIECES
    width = days // count
    firsts = [pl.multiple_of(((1 - core) if p < count // 2 else core) * (days // 2) + p % (count // 2) * width, width) for p in range(count)]
    pairs = [(res_any.at[:, pl.ds(firsts[p], width)], res_ref.at[columns(p, width)]) for p in range(count)]
    return bring(pairs, sems), firsts[::PIECES]


def first_kernel(
    start_any, factor_any, ids_any, bits_any, res_any,
    out_ref, wide_ref, tall_ref,
    start_ref, factor_ref, ids_ref, bits_ref, res_ref, total_ref, sems,
):
    copies, factors, width = out_ref.shape
    firms, days = res_ref.shape
    n = total_ref.shape[1]
    pairs = [(start_any, start_ref), (factor_any, factor_ref), (ids_any, ids_ref), (bits_any, bits_ref)]
    small = [pltpu.make_async_copy(a, b, sems.at[STEPS * PIECES + i]) for i, (a, b) in enumerate(pairs)]
    for copy in small:
        copy.start()
    tiles = [columns(t, days // STEPS) for t in range(STEPS)]
    large = bring(piece_pairs(res_any, res_ref, columns), sems)
    for copy in small:
        copy.wait()
    start = start_ref[...]
    high = start.astype(jnp.bfloat16).astype(jnp.float32)
    both = jnp.concatenate([high, start - high, jnp.zeros((n - 2 * factors, days), jnp.float32)], axis=0)
    both = both.T.astype(jnp.bfloat16)
    mixed = corners(fast(stack(start, "hl"), stack(factor_ref[...], "hl"), NT), factors, factors)
    mixed = jnp.concatenate([mixed, jnp.zeros((factors, width - firms - factors), jnp.float32)], axis=1)
    out_ref[:, :, firms:] = jnp.broadcast_to(mixed[None], (copies, factors, width - firms))
    put_signs(ids_ref, bits_ref, wide_ref, tall_ref)
    for t in range(STEPS):
        arrive(large, t)
        high, low = split(res_ref[tiles[t]])
        right = both[t * (days // STEPS) : (t + 1) * (days // STEPS)]
        part = fast(high, right, NN) + fast(low, right, NN)
        total_ref[...] = part if t == 0 else total_ref[...] + part
    total = total_ref[...].T
    total = total[0:factors] + total[factors : 2 * factors]
    out_ref[:, :, 0:firms] = jnp.broadcast_to(total[None], (copies, factors, firms))


def days_from(raw_t, signs_ref, loadings_ref, factor_ref, left_ref, small_ref, right_ref):
    factors = loadings_ref.shape[0]
    n = raw_t.shape[0]
    high, middle, low = split3(raw_t)
    signs = signs_ref[...]
    left_ref[0:n] = (signs * high.astype(jnp.float32)).astype(jnp.bfloat16)
    left_ref[n:] = (signs * middle.astype(jnp.float32)).astype(jnp.bfloat16)
    both = jnp.concatenate([high, middle], axis=0)
    small = corners(fast(stack(loadings_ref[...], "hl"), both, NT), factors, n)
    small_ref[...] = stack(small, "hhl0")
    right_ref[...] = stack(factor_ref[...], "hlh0")
    return compact(gram_of(high, middle, low, NT, 0), factors)


def days_tiles(copies, firsts, res_ref, left_ref, small_ref, right_ref, send_ref, keep_ref):
    n = small_ref.shape[1]
    rows = send_ref.shape[1] - small_ref.shape[0] // 4
    width = res_ref.shape[1] // STEPS
    half = STEPS // 2
    for t in range(STEPS):
        arrive(copies, t)
        high, low = split(res_ref[columns(t, width)])
        both = fast(left_ref[...], high, NN)
        more = fast(small_ref[...], right_ref[:, pl.ds(firsts[t], width)], TN)
        tile = both[0:n] + both[n:] + fast(left_ref[0:n], low, NN) + more
        out_ref = send_ref if t < half else keep_ref
        at = slice(t % half * (width // rows), (t % half + 1) * (width // rows))
        out_ref[at, 0:rows, :] = tile.T.reshape(width // rows, rows, n)


def put_gram(gram, send_ref, keep_ref):
    copies, rows, n = send_ref.shape
    wide = jnp.broadcast_to(gram[None], (copies, gram.shape[0], n))
    send_ref[:, rows - gram.shape[0] :, :] = wide
    keep_ref[:, rows - gram.shape[0] :, :] = wide


def days_first_kernel(core_ref, got_ref, signs_ref, loadings_ref, factor_ref, res_any, send_ref, keep_ref, left_ref, small_ref, right_ref, res_ref, sems):
    copies, firsts = bring_for_core(core_ref[0], res_any, res_ref, sems)
    factors, firms = loadings_ref.shape
    n = signs_ref.shape[0]
    got = got_ref[...].sum(axis=0)
    by_residuals, mixed = got[:, 0:firms], got[:, firms : firms + factors]
    by_factors = jnp.zeros((factors, firms), jnp.float32)
    for m in range(factors):
        by_factors = by_factors + mixed[:, m : m + 1] * loadings_ref[m : m + 1, :]
    reps = n // factors
    raw_t = signs_ref[...] * jnp.concatenate([by_residuals] * reps, axis=0)
    raw_t = raw_t + jnp.concatenate([by_factors] * reps, axis=0)
    put_gram(days_from(raw_t, signs_ref, loadings_ref, factor_ref, left_ref, small_ref, right_ref), send_ref, keep_ref)
    days_tiles(copies, firsts, res_ref, left_ref, small_ref, right_ref, send_ref, keep_ref)


def days_later_kernel(core_ref, got_ref, signs_ref, loadings_ref, factor_ref, res_any, send_ref, keep_ref, left_ref, small_ref, right_ref, res_ref, sems):
    copies, firsts = bring_for_core(core_ref[0], res_any, res_ref, sems)
    put_gram(days_from(got_ref[...].T, signs_ref, loadings_ref, factor_ref, left_ref, small_ref, right_ref), send_ref, keep_ref)
    days_tiles(copies, firsts, res_ref, left_ref, small_ref, right_ref, send_ref, keep_ref)


def firms_kernel(core_ref, mine_ref, other_ref, signs_ref, loadings_ref, factor_ref, res_any, out_ref, raw_ref, right_ref, add_ref, res_ref, sems):
    factors = loadings_ref.shape[0]
    half, n = mine_ref.shape
    rows = res_ref.shape[0] // STEPS
    large = bring(piece_pairs(res_any, res_ref, rows_of), sems)
    core = core_ref[0]
    raw_ref[pl.ds(pl.multiple_of(core * half, half), half), :] = mine_ref[...]
    raw_ref[pl.ds(pl.multiple_of((1 - core) * half, half), half), :] = other_ref[...]
    raw = raw_ref[...]
    high, middle, low = split3(raw)
    right_ref[:, 0:n] = high
    right_ref[:, n:] = middle
    gram = compact(gram_of(high, middle, low, TN, 1), factors)
    copies, total = out_ref.shape[0], out_ref.shape[1]
    out_ref[:, total - factors :, :] = jnp.broadcast_to(gram[None], (copies, factors, n))
    small = corners(fast(stack(factor_ref[...], "hl"), right_ref[...], NN), factors, n)
    add_ref[...] = fast(stack(loadings_ref[...], "hlh0"), stack(small, "hhl0"), TN)
    block = total - factors
    for t in range(STEPS):
        arrive(large, t)
        at = slice(t * rows, (t + 1) * rows)
        high, low = split(res_ref[at, :])
        both = fast(high, right_ref[...], NN)
        part = both[:, 0:n] + both[:, n:] + fast(low, right_ref[:, 0:n], NN)
        part = signs_ref[at, :] * part + add_ref[at, :]
        out_ref[t * rows // block : (t + 1) * rows // block, 0:block, :] = part.reshape(rows // block, block, n)


def turn_kernel(got_ref, out_ref, inverse_ref):
    copies, rows, _ = out_ref.shape
    total = got_ref[...].sum(axis=0)
    inverse = inverse_blocks(total[rows:], total.shape[0] - rows)
    inverse_ref[...] = inverse
    chunk = exact(total[0:rows], inverse, NT)
    out_ref[...] = jnp.broadcast_to(chunk[None], out_ref.shape)


def last_kernel(core_ref, mine_ref, other_ref, raw_ref, out_ref):
    half = mine_ref.shape[0]
    mine, other = mine_ref[...], other_ref[...]
    core = core_ref[0]
    raw_ref[pl.ds(pl.multiple_of(core * half, half), half), :] = mine
    raw_ref[pl.ds(pl.multiple_of((1 - core) * half, half), half), :] = other
    gram = compact(gram_of(*split3(mine), TN, 1) + gram_of(*split3(other), TN, 1), out_ref.shape[1])
    out_ref[...] = jnp.broadcast_to(gram[None], out_ref.shape)


def loadings_kernel(raw_ref, inverse_ref, out_ref, *, scale):
    out_ref[...] = rotated(raw_ref[...], scale * inverse_ref[...])


def factors_kernel(got_ref, raw_ref, out_ref, *, scale):
    gram = got_ref[...].sum(axis=0)
    out_ref[...] = rotated(raw_ref[...], scale * inverse_blocks(gram, gram.shape[0]))


def shape(*dims):
    return jax.ShapeDtypeStruct(dims, jnp.float32)


def inputs(count):
    small = [pl.BlockSpec(memory_space=pltpu.VMEM)] * count
    return [pl.BlockSpec(memory_space=pltpu.SMEM), *small]


def in_hbm(x):
    return pltpu.with_memory_space_constraint(x, pltpu.HBM)


def on_device(residuals, loadings, factor_path, start_guess, cluster_ids, sign_bits, *, chips, total_firms, total_days, day_ranks):
    firms, days = residuals.shape
    factors = start_guess.shape[1]
    clusters, reps = sign_bits.shape
    n = reps * factors
    half = days // 2
    chunk = half // chips
    block = firms // day_ranks
    loadings_t, factor_t, start_t = loadings.T, factor_path.T, start_guess.T
    core = lax.axis_index("core").astype(jnp.int32).reshape(1)

    residuals = in_hbm(residuals)
    block_scratch = [pltpu.VMEM((firms, days), jnp.float32), pltpu.SemaphoreType.DMA((STEPS * PIECES,))]
    first, signs_t, signs = pl.pallas_call(
        first_kernel,
        in_specs=[pl.BlockSpec(memory_space=pl.ANY)] * 5,
        out_shape=(
            shape(day_ranks, factors, firms + n),
            shape(n, firms),
            shape(firms, n),
        ),
        scratch_shapes=[
            pltpu.VMEM((factors, days), jnp.float32),
            pltpu.VMEM((factors, days), jnp.float32),
            pltpu.VMEM((1, firms), jnp.int32),
            pltpu.VMEM((reps, clusters), jnp.int32),
            pltpu.VMEM((firms, days), jnp.float32),
            pltpu.VMEM((firms, n), jnp.float32),
            pltpu.SemaphoreType.DMA((STEPS * PIECES + 4,)),
        ],
        compiler_params=PARAMS,
        name="first",
    )(in_hbm(start_t), in_hbm(factor_t), in_hbm(cluster_ids.reshape(1, firms)), in_hbm(sign_bits.T), residuals)
    first = lax.all_to_all(first, ("x_hi", "y"), 0, 0, tiled=True)

    day_scratch = [
        pltpu.VMEM((2 * n, firms), jnp.bfloat16),
        pltpu.VMEM((4 * factors, n), jnp.bfloat16),
        pltpu.VMEM((4 * factors, days), jnp.bfloat16),
        *block_scratch,
    ]
    parts = (chips, chunk + factors, n)

    def turn(got, rows):
        return pl.pallas_call(
            turn_kernel,
            out_shape=(shape(got.shape[0], rows, n), shape(n, n)),
            compiler_params=PARAMS,
            name="turn",
        )(got)

    def sum_firms(send, keep):
        pair = keep + lax.ppermute(send, "core", [(0, 1), (1, 0)])
        mine, inverse = turn(lax.all_to_all(pair, ("x_lo", "z"), 0, 0, tiled=True), chunk)
        mine = lax.all_to_all(mine, ("x_lo", "z"), 0, 0, tiled=True).reshape(half, n)
        return mine, lax.ppermute(mine, "core", [(0, 1), (1, 0)]), inverse

    send, keep = pl.pallas_call(
        days_first_kernel,
        in_specs=inputs(4) + [pl.BlockSpec(memory_space=pl.ANY)],
        scratch_shapes=day_scratch,
        out_shape=(shape(*parts), shape(*parts)),
        compiler_params=PARAMS,
        name="days_first",
    )(core, first, signs_t, loadings_t, factor_t, residuals)
    mine, other, _ = sum_firms(send, keep)

    by_day = pl.pallas_call(
        firms_kernel,
        in_specs=inputs(5) + [pl.BlockSpec(memory_space=pl.ANY)],
        scratch_shapes=[
            pltpu.VMEM((days, n), jnp.float32),
            pltpu.VMEM((days, 2 * n), jnp.bfloat16),
            pltpu.VMEM((firms, n), jnp.float32),
            *block_scratch,
        ],
        out_shape=shape(day_ranks, block + factors, n),
        compiler_params=PARAMS,
        name="firms",
    )(core, mine, other, signs, loadings_t, factor_t, residuals)
    raw_loads, _ = turn(lax.all_to_all(by_day, ("x_hi", "y"), 0, 0, tiled=True), block)
    raw_loads = lax.all_to_all(raw_loads, ("x_hi", "y"), 0, 0, tiled=True).reshape(firms, n)

    send, keep = pl.pallas_call(
        days_later_kernel,
        in_specs=inputs(4) + [pl.BlockSpec(memory_space=pl.ANY)],
        scratch_shapes=day_scratch,
        out_shape=(shape(*parts), shape(*parts)),
        compiler_params=PARAMS,
        name="days_later",
    )(core, raw_loads, signs_t, loadings_t, factor_t, residuals)
    mine, other, inverse = sum_firms(send, keep)

    raw_factors, last = pl.pallas_call(
        last_kernel,
        in_specs=inputs(2),
        out_shape=(shape(days, n), shape(day_ranks, factors, n)),
        compiler_params=PARAMS,
        name="last",
    )(core, mine, other)
    last = lax.all_to_all(last, ("x_hi", "y"), 0, 0, tiled=True)
    boot_loadings = pl.pallas_call(
        functools.partial(loadings_kernel, scale=math.sqrt(total_firms)),
        out_shape=shape(firms, n),
        compiler_params=PARAMS,
        name="boot_loadings",
    )(raw_loads, inverse)
    boot_factors = pl.pallas_call(
        functools.partial(factors_kernel, scale=math.sqrt(total_days)),
        out_shape=shape(days, n),
        compiler_params=PARAMS,
        name="boot_factors",
    )(last, raw_factors)
    return boot_loadings, boot_factors


def solution(mesh):
    firm_ranks, day_ranks = mesh.shape["firm"], mesh.shape["day"]
    axes = ("x_lo", "z", "core", "x_hi", "y")
    fine = Mesh(mesh.devices.reshape(2, firm_ranks // 4, 2, 2, day_ranks // 2), axes)
    firm, day = ("x_lo", "z", "core"), ("x_hi", "y")

    def run(residuals, *rest):
        total_firms, total_days = residuals.shape
        body = functools.partial(
            on_device, chips=firm_ranks // 2, total_firms=total_firms, total_days=total_days, day_ranks=day_ranks
        )
        return jax.shard_map(
            body,
            mesh=fine,
            in_specs=(P(firm, day), P(firm, None), P(day, None), P(day, None), P(firm), P()),
            out_specs=(P(firm, None), P(day, None)),
            check_vma=False,
        )(residuals, *rest)

    return run
```

```python
import functools
import math

import jax
import jax.numpy as jnp
from jax import lax
from jax.experimental import pallas as pl
from jax.experimental.pallas import tpu as pltpu
from jax.sharding import Mesh
from jax.sharding import PartitionSpec as P

STEPS = 4
PIECES = 2
AHEAD = 8
HIGHEST = lax.Precision.HIGHEST
NN = (((1,), (0,)), ((), ()))
NT = (((1,), (1,)), ((), ()))
TN = (((0,), (0,)), ((), ()))
PARAMS = pltpu.CompilerParams(vmem_limit_bytes=32 * 1024 * 1024)


def exact(a, b, dims):
    return lax.dot_general(a, b, dims, precision=HIGHEST, preferred_element_type=jnp.float32)


def fast(a, b, dims):
    return lax.dot_general(a, b, dims, preferred_element_type=jnp.float32)


def split(x):
    high = x.astype(jnp.bfloat16)
    return high, (x - high.astype(jnp.float32)).astype(jnp.bfloat16)


def split3(x):
    high = x.astype(jnp.bfloat16)
    rest = x - high.astype(jnp.float32)
    middle = rest.astype(jnp.bfloat16)
    return high, middle, (rest - middle.astype(jnp.float32)).astype(jnp.bfloat16)


def corners(both, rows, cols):
    return both[:rows, :cols] + (both[:rows, cols:] + both[rows:, :cols] + both[rows:, cols:])


def gram_of(high, middle, low, dims, axis):
    both = jnp.concatenate([high, middle], axis=axis)
    n = both.shape[axis] // 2
    cross = fast(high, low, dims)
    return corners(fast(both, both, dims), n, n) + (cross + cross.T)


def stack(x, order):
    high = x.astype(jnp.bfloat16).astype(jnp.float32)
    parts = {"h": high, "l": x - high, "0": jnp.zeros_like(x)}
    return jnp.concatenate([parts[p] for p in order], axis=0).astype(jnp.bfloat16)


def rotated(x, inverse):
    n = inverse.shape[0]
    high, low = split(x)
    top, rest = split(inverse.T)
    right = jnp.concatenate(
        [jnp.concatenate([top, rest], axis=1), jnp.concatenate([top, jnp.zeros_like(rest)], axis=1)], axis=0
    )
    both = fast(jnp.concatenate([high, low], axis=1), right, NN)
    return both[:, 0:n] + both[:, n:]


def compact(full, factors):
    n = full.shape[0]
    row = lax.broadcasted_iota(jnp.int32, (n, n), 0) // factors
    lane = lax.broadcasted_iota(jnp.int32, (n, n), 1) // factors
    kept = jnp.where(row == lane, full, 0.0)
    return kept.reshape(n // factors, factors, n).sum(axis=0)


def inverse_blocks(gram, factors):
    n = gram.shape[1]
    row = lax.broadcasted_iota(jnp.int32, (factors, n), 0)
    lane = lax.broadcasted_iota(jnp.int32, (factors, n), 1)
    first = (lane // factors) * factors
    rest = gram
    inverse = jnp.where(row == lane - first, 1.0, 0.0)
    for j in range(factors):
        column = jnp.take_along_axis(rest, first + j, axis=1, mode="promise_in_bounds")
        pivot = column[j : j + 1]
        ratio = jnp.where(row > j, column / pivot, 0.0)
        rest = rest - ratio * rest[j : j + 1]
        inverse = inverse - ratio * inverse[j : j + 1]
        inverse = jnp.where(row == j, inverse / jnp.sqrt(pivot), inverse)
    wide = jnp.concatenate([inverse] * (n // factors), axis=0)
    row = lax.broadcasted_iota(jnp.int32, (n, n), 0) // factors
    lane = lax.broadcasted_iota(jnp.int32, (n, n), 1) // factors
    return jnp.where(row == lane, wide, 0.0)


def signs_kernel(ids_ref, bits_ref, wide_ref, tall_ref):
    reps, clusters = bits_ref.shape
    n, firms = wide_ref.shape
    table = 2.0 * bits_ref[...].astype(jnp.float32) - 1.0
    table = jnp.broadcast_to(table[:, None, :], (reps, n // reps, clusters))
    table = table.reshape(n, clusters).astype(jnp.bfloat16)
    cluster = lax.broadcasted_iota(jnp.int32, (clusters, firms), 0)
    member = jnp.where(cluster == ids_ref[...], 1.0, 0.0).astype(jnp.bfloat16)
    wide = fast(table, member, NN)
    wide_ref[...] = wide
    tall_ref[...] = wide.T


def columns(t, width):
    return (slice(None), slice(t * width, (t + 1) * width))


def rows_of(t, rows):
    return (slice(t * rows, (t + 1) * rows), slice(None))


def bring(pairs, sems):
    copies = [pltpu.make_async_copy(a, b, sems.at[t]) for t, (a, b) in enumerate(pairs)]
    for copy in copies[:AHEAD]:
        copy.start()
    return copies


def arrive(copies, t):
    for p in range(t * PIECES, (t + 1) * PIECES):
        copies[p].wait()
        if p + AHEAD < len(copies):
            copies[p + AHEAD].start()


def piece_pairs(res_any, res_ref, piece):
    size = res_ref.shape[1] if piece is columns else res_ref.shape[0]
    count = STEPS * PIECES
    return [(res_any.at[piece(p, size // count)], res_ref.at[piece(p, size // count)]) for p in range(count)]


def bring_for_core(core, res_any, res_ref, sems):
    days = res_ref.shape[1]
    count = STEPS * PIECES
    width = days // count
    firsts = [pl.multiple_of(((1 - core) if p < count // 2 else core) * (days // 2) + p % (count // 2) * width, width) for p in range(count)]
    pairs = [(res_any.at[:, pl.ds(firsts[p], width)], res_ref.at[columns(p, width)]) for p in range(count)]
    return bring(pairs, sems), firsts[::PIECES]


def first_kernel(
    start_any, factor_any, res_any,
    out_ref,
    start_ref, factor_ref, res_ref, total_ref, sems,
):
    copies, factors, width = out_ref.shape
    firms, days = res_ref.shape
    n = total_ref.shape[1]
    pairs = [(start_any, start_ref), (factor_any, factor_ref)]
    small = [pltpu.make_async_copy(a, b, sems.at[STEPS * PIECES + i]) for i, (a, b) in enumerate(pairs)]
    for copy in small:
        copy.start()
    tiles = [columns(t, days // STEPS) for t in range(STEPS)]
    large = bring(piece_pairs(res_any, res_ref, columns), sems)
    for copy in small:
        copy.wait()
    start = start_ref[...]
    high = start.astype(jnp.bfloat16).astype(jnp.float32)
    both = jnp.concatenate([high, start - high, jnp.zeros((n - 2 * factors, days), jnp.float32)], axis=0)
    both = both.T.astype(jnp.bfloat16)
    mixed = corners(fast(stack(start, "hl"), stack(factor_ref[...], "hl"), NT), factors, factors)
    mixed = jnp.concatenate([mixed, jnp.zeros((factors, width - firms - factors), jnp.float32)], axis=1)
    out_ref[:, :, firms:] = jnp.broadcast_to(mixed[None], (copies, factors, width - firms))
    for t in range(STEPS):
        arrive(large, t)
        high, low = split(res_ref[tiles[t]])
        right = both[t * (days // STEPS) : (t + 1) * (days // STEPS)]
        part = fast(high, right, NN) + fast(low, right, NN)
        total_ref[...] = part if t == 0 else total_ref[...] + part
    total = total_ref[...].T
    total = total[0:factors] + total[factors : 2 * factors]
    out_ref[:, :, 0:firms] = jnp.broadcast_to(total[None], (copies, factors, firms))


def days_from(raw_t, signs_ref, loadings_ref, factor_ref, left_ref, small_ref, right_ref):
    factors = loadings_ref.shape[0]
    n = raw_t.shape[0]
    high, middle, low = split3(raw_t)
    signs = signs_ref[...]
    left_ref[0:n] = (signs * high.astype(jnp.float32)).astype(jnp.bfloat16)
    left_ref[n:] = (signs * middle.astype(jnp.float32)).astype(jnp.bfloat16)
    both = jnp.concatenate([high, middle], axis=0)
    small = corners(fast(stack(loadings_ref[...], "hl"), both, NT), factors, n)
    small_ref[...] = stack(small, "hhl0")
    right_ref[...] = stack(factor_ref[...], "hlh0")
    return compact(gram_of(high, middle, low, NT, 0), factors)


def days_tiles(copies, firsts, res_ref, left_ref, small_ref, right_ref, send_ref, keep_ref):
    n = small_ref.shape[1]
    rows = send_ref.shape[1] - small_ref.shape[0] // 4
    width = res_ref.shape[1] // STEPS
    half = STEPS // 2
    for t in range(STEPS):
        arrive(copies, t)
        high, low = split(res_ref[columns(t, width)])
        both = fast(left_ref[...], high, NN)
        more = fast(small_ref[...], right_ref[:, pl.ds(firsts[t], width)], TN)
        tile = both[0:n] + both[n:] + fast(left_ref[0:n], low, NN) + more
        out_ref = send_ref if t < half else keep_ref
        at = slice(t % half * (width // rows), (t % half + 1) * (width // rows))
        out_ref[at, 0:rows, :] = tile.T.reshape(width // rows, rows, n)


def put_gram(gram, send_ref, keep_ref):
    copies, rows, n = send_ref.shape
    wide = jnp.broadcast_to(gram[None], (copies, gram.shape[0], n))
    send_ref[:, rows - gram.shape[0] :, :] = wide
    keep_ref[:, rows - gram.shape[0] :, :] = wide


def days_first_kernel(core_ref, got_ref, signs_ref, loadings_ref, factor_ref, res_any, send_ref, keep_ref, left_ref, small_ref, right_ref, res_ref, sems):
    copies, firsts = bring_for_core(core_ref[0], res_any, res_ref, sems)
    factors, firms = loadings_ref.shape
    n = signs_ref.shape[0]
    got = got_ref[...].sum(axis=0)
    by_residuals, mixed = got[:, 0:firms], got[:, firms : firms + factors]
    by_factors = jnp.zeros((factors, firms), jnp.float32)
    for m in range(factors):
        by_factors = by_factors + mixed[:, m : m + 1] * loadings_ref[m : m + 1, :]
    reps = n // factors
    raw_t = signs_ref[...] * jnp.concatenate([by_residuals] * reps, axis=0)
    raw_t = raw_t + jnp.concatenate([by_factors] * reps, axis=0)
    put_gram(days_from(raw_t, signs_ref, loadings_ref, factor_ref, left_ref, small_ref, right_ref), send_ref, keep_ref)
    days_tiles(copies, firsts, res_ref, left_ref, small_ref, right_ref, send_ref, keep_ref)


def days_later_kernel(core_ref, got_ref, signs_ref, loadings_ref, factor_ref, res_any, send_ref, keep_ref, left_ref, small_ref, right_ref, res_ref, sems):
    copies, firsts = bring_for_core(core_ref[0], res_any, res_ref, sems)
    put_gram(days_from(got_ref[...].T, signs_ref, loadings_ref, factor_ref, left_ref, small_ref, right_ref), send_ref, keep_ref)
    days_tiles(copies, firsts, res_ref, left_ref, small_ref, right_ref, send_ref, keep_ref)


def firms_kernel(core_ref, mine_ref, other_ref, signs_ref, loadings_ref, factor_ref, res_any, out_ref, raw_ref, right_ref, add_ref, res_ref, sems):
    factors = loadings_ref.shape[0]
    half, n = mine_ref.shape
    rows = res_ref.shape[0] // STEPS
    large = bring(piece_pairs(res_any, res_ref, rows_of), sems)
    core = core_ref[0]
    raw_ref[pl.ds(pl.multiple_of(core * half, half), half), :] = mine_ref[...]
    raw_ref[pl.ds(pl.multiple_of((1 - core) * half, half), half), :] = other_ref[...]
    raw = raw_ref[...]
    high, middle, low = split3(raw)
    right_ref[:, 0:n] = high
    right_ref[:, n:] = middle
    gram = compact(gram_of(high, middle, low, TN, 1), factors)
    copies, total = out_ref.shape[0], out_ref.shape[1]
    out_ref[:, total - factors :, :] = jnp.broadcast_to(gram[None], (copies, factors, n))
    small = corners(fast(stack(factor_ref[...], "hl"), right_ref[...], NN), factors, n)
    add_ref[...] = fast(stack(loadings_ref[...], "hlh0"), stack(small, "hhl0"), TN)
    block = total - factors
    for t in range(STEPS):
        arrive(large, t)
        at = slice(t * rows, (t + 1) * rows)
        high, low = split(res_ref[at, :])
        both = fast(high, right_ref[...], NN)
        part = both[:, 0:n] + both[:, n:] + fast(low, right_ref[:, 0:n], NN)
        part = signs_ref[at, :] * part + add_ref[at, :]
        out_ref[t * rows // block : (t + 1) * rows // block, 0:block, :] = part.reshape(rows // block, block, n)


def turn_kernel(got_ref, out_ref, *inverse_ref):
    copies, rows, _ = out_ref.shape
    total = got_ref[...].sum(axis=0)
    inverse = inverse_blocks(total[rows:], total.shape[0] - rows)
    for ref in inverse_ref:
        ref[...] = inverse
    chunk = exact(total[0:rows], inverse, NT)
    out_ref[...] = jnp.broadcast_to(chunk[None], out_ref.shape)


def last_kernel(core_ref, mine_ref, other_ref, raw_ref, out_ref):
    half = mine_ref.shape[0]
    mine, other = mine_ref[...], other_ref[...]
    core = core_ref[0]
    raw_ref[pl.ds(pl.multiple_of(core * half, half), half), :] = mine
    raw_ref[pl.ds(pl.multiple_of((1 - core) * half, half), half), :] = other
    gram = compact(gram_of(*split3(mine), TN, 1) + gram_of(*split3(other), TN, 1), out_ref.shape[1])
    out_ref[...] = jnp.broadcast_to(gram[None], out_ref.shape)


def loadings_kernel(raw_ref, inverse_ref, out_ref, *, scale):
    out_ref[...] = rotated(raw_ref[...], scale * inverse_ref[...])


def factors_kernel(got_ref, raw_ref, out_ref, *, scale):
    gram = got_ref[...].sum(axis=0)
    out_ref[...] = rotated(raw_ref[...], scale * inverse_blocks(gram, gram.shape[0]))


def shape(*dims):
    return jax.ShapeDtypeStruct(dims, jnp.float32)


def inputs(count):
    small = [pl.BlockSpec(memory_space=pltpu.VMEM)] * count
    return [pl.BlockSpec(memory_space=pltpu.SMEM), *small]


def in_hbm(x):
    return pltpu.with_memory_space_constraint(x, pltpu.HBM)


def on_device(residuals, loadings, factor_path, start_guess, cluster_ids, sign_bits, *, chips, total_firms, total_days, day_ranks):
    firms, days = residuals.shape
    factors = start_guess.shape[1]
    clusters, reps = sign_bits.shape
    n = reps * factors
    half = days // 2
    chunk = half // chips
    block = firms // day_ranks
    loadings_t, factor_t, start_t = loadings.T, factor_path.T, start_guess.T
    core = lax.axis_index("core").astype(jnp.int32).reshape(1)

    residuals = in_hbm(residuals)
    block_scratch = [pltpu.VMEM((firms, days), jnp.float32), pltpu.SemaphoreType.DMA((STEPS * PIECES,))]
    first = pl.pallas_call(
        first_kernel,
        in_specs=[pl.BlockSpec(memory_space=pl.ANY)] * 3,
        out_shape=shape(day_ranks, factors, firms + n),
        scratch_shapes=[
            pltpu.VMEM((factors, days), jnp.float32),
            pltpu.VMEM((factors, days), jnp.float32),
            pltpu.VMEM((firms, days), jnp.float32),
            pltpu.VMEM((firms, n), jnp.float32),
            pltpu.SemaphoreType.DMA((STEPS * PIECES + 2,)),
        ],
        compiler_params=PARAMS,
        name="first",
    )(in_hbm(start_t), in_hbm(factor_t), residuals)
    signs_t, signs = pl.pallas_call(
        signs_kernel,
        out_shape=(shape(n, firms), shape(firms, n)),
        compiler_params=PARAMS,
        name="signs",
    )(cluster_ids.reshape(1, firms), sign_bits.T)
    first = lax.all_to_all(first, ("x_hi", "y"), 0, 0, tiled=True)

    day_scratch = [
        pltpu.VMEM((2 * n, firms), jnp.bfloat16),
        pltpu.VMEM((4 * factors, n), jnp.bfloat16),
        pltpu.VMEM((4 * factors, days), jnp.bfloat16),
        *block_scratch,
    ]
    parts = (chips, chunk + factors, n)

    def turn(got, rows, with_inverse):
        out = shape(got.shape[0], rows, n)
        return pl.pallas_call(
            turn_kernel,
            out_shape=(out, shape(n, n)) if with_inverse else out,
            compiler_params=PARAMS,
            name="turn",
        )(got)

    def scatter_firms(send, keep):
        pair = keep + lax.ppermute(send, "core", [(0, 1), (1, 0)])
        return lax.all_to_all(pair, ("x_lo", "z"), 0, 0, tiled=True)

    def gather_firms(mine):
        mine = lax.all_to_all(mine, ("x_lo", "z"), 0, 0, tiled=True).reshape(half, n)
        return mine, lax.ppermute(mine, "core", [(0, 1), (1, 0)])

    send, keep = pl.pallas_call(
        days_first_kernel,
        in_specs=inputs(4) + [pl.BlockSpec(memory_space=pl.ANY)],
        scratch_shapes=day_scratch,
        out_shape=(shape(*parts), shape(*parts)),
        compiler_params=PARAMS,
        name="days_first",
    )(core, first, signs_t, loadings_t, factor_t, residuals)
    mine, other = gather_firms(turn(scatter_firms(send, keep), chunk, False))

    by_day = pl.pallas_call(
        firms_kernel,
        in_specs=inputs(5) + [pl.BlockSpec(memory_space=pl.ANY)],
        scratch_shapes=[
            pltpu.VMEM((days, n), jnp.float32),
            pltpu.VMEM((days, 2 * n), jnp.bfloat16),
            pltpu.VMEM((firms, n), jnp.float32),
            *block_scratch,
        ],
        out_shape=shape(day_ranks, block + factors, n),
        compiler_params=PARAMS,
        name="firms",
    )(core, mine, other, signs, loadings_t, factor_t, residuals)
    raw_loads = turn(lax.all_to_all(by_day, ("x_hi", "y"), 0, 0, tiled=True), block, False)
    raw_loads = lax.all_to_all(raw_loads, ("x_hi", "y"), 0, 0, tiled=True).reshape(firms, n)

    send, keep = pl.pallas_call(
        days_later_kernel,
        in_specs=inputs(4) + [pl.BlockSpec(memory_space=pl.ANY)],
        scratch_shapes=day_scratch,
        out_shape=(shape(*parts), shape(*parts)),
        compiler_params=PARAMS,
        name="days_later",
    )(core, raw_loads, signs_t, loadings_t, factor_t, residuals)
    mine, inverse = turn(scatter_firms(send, keep), chunk, True)
    mine, other = gather_firms(mine)

    raw_factors, last = pl.pallas_call(
        last_kernel,
        in_specs=inputs(2),
        out_shape=(shape(days, n), shape(day_ranks, factors, n)),
        compiler_params=PARAMS,
        name="last",
    )(core, mine, other)
    boot_loadings = pl.pallas_call(
        functools.partial(loadings_kernel, scale=math.sqrt(total_firms)),
        out_shape=shape(firms, n),
        compiler_params=PARAMS,
        name="boot_loadings",
    )(raw_loads, inverse)
    last, boot_loadings = lax.optimization_barrier((last, boot_loadings))
    last = lax.all_to_all(last, ("x_hi", "y"), 0, 0, tiled=True)
    boot_factors = pl.pallas_call(
        functools.partial(factors_kernel, scale=math.sqrt(total_days)),
        out_shape=shape(days, n),
        compiler_params=PARAMS,
        name="boot_factors",
    )(last, raw_factors)
    return boot_loadings, boot_factors


def solution(mesh):
    firm_ranks, day_ranks = mesh.shape["firm"], mesh.shape["day"]
    axes = ("x_lo", "z", "core", "x_hi", "y")
    fine = Mesh(mesh.devices.reshape(2, firm_ranks // 4, 2, 2, day_ranks // 2), axes)
    firm, day = ("x_lo", "z", "core"), ("x_hi", "y")

    def run(residuals, *rest):
        total_firms, total_days = residuals.shape
        body = functools.partial(
            on_device, chips=firm_ranks // 2, total_firms=total_firms, total_days=total_days, day_ranks=day_ranks
        )
        return jax.shard_map(
            body,
            mesh=fine,
            in_specs=(P(firm, day), P(firm, None), P(day, None), P(day, None), P(firm), P()),
            out_specs=(P(firm, None), P(day, None)),
            check_vma=False,
        )(residuals, *rest)

    return run
```

```python
import functools
import math

import jax
import jax.numpy as jnp
from jax import lax
from jax.experimental import pallas as pl
from jax.experimental.pallas import tpu as pltpu
from jax.sharding import Mesh
from jax.sharding import PartitionSpec as P

STEPS = 4
PIECES = 2
AHEAD = 8
HIGHEST = lax.Precision.HIGHEST
NN = (((1,), (0,)), ((), ()))
NT = (((1,), (1,)), ((), ()))
TN = (((0,), (0,)), ((), ()))
PARAMS = pltpu.CompilerParams(vmem_limit_bytes=32 * 1024 * 1024)


def exact(a, b, dims):
    return lax.dot_general(a, b, dims, precision=HIGHEST, preferred_element_type=jnp.float32)


def fast(a, b, dims):
    return lax.dot_general(a, b, dims, preferred_element_type=jnp.float32)


def split(x):
    high = x.astype(jnp.bfloat16)
    return high, (x - high.astype(jnp.float32)).astype(jnp.bfloat16)


def split3(x):
    high = x.astype(jnp.bfloat16)
    rest = x - high.astype(jnp.float32)
    middle = rest.astype(jnp.bfloat16)
    return high, middle, (rest - middle.astype(jnp.float32)).astype(jnp.bfloat16)


def corners(both, rows, cols):
    return both[:rows, :cols] + (both[:rows, cols:] + both[rows:, :cols] + both[rows:, cols:])


def gram_of(high, middle, low, dims, axis):
    both = jnp.concatenate([high, middle], axis=axis)
    n = both.shape[axis] // 2
    cross = fast(high, low, dims)
    return corners(fast(both, both, dims), n, n) + (cross + cross.T)


def stack(x, order):
    high = x.astype(jnp.bfloat16).astype(jnp.float32)
    parts = {"h": high, "l": x - high, "0": jnp.zeros_like(x)}
    return jnp.concatenate([parts[p] for p in order], axis=0).astype(jnp.bfloat16)


def turning(inverse):
    top, rest = split(inverse.T)
    return jnp.concatenate(
        [jnp.concatenate([top, rest], axis=1), jnp.concatenate([top, jnp.zeros_like(rest)], axis=1)], axis=0
    )


def rotated(x, right):
    n = x.shape[1]
    both = fast(jnp.concatenate(split(x), axis=1), right, NN)
    return both[:, 0:n] + both[:, n:]


def compact(full, factors):
    n = full.shape[0]
    row = lax.broadcasted_iota(jnp.int32, (n, n), 0) // factors
    lane = lax.broadcasted_iota(jnp.int32, (n, n), 1) // factors
    kept = jnp.where(row == lane, full, 0.0)
    return kept.reshape(n // factors, factors, n).sum(axis=0)


def inverse_blocks(gram, factors):
    n = gram.shape[1]
    row = lax.broadcasted_iota(jnp.int32, (factors, n), 0)
    lane = lax.broadcasted_iota(jnp.int32, (factors, n), 1)
    first = (lane // factors) * factors
    inverse = jnp.where(row == lane - first, 1.0, 0.0)
    spread = [jnp.take_along_axis(gram, first + j, axis=1, mode="promise_in_bounds") for j in range(factors)]
    for j in range(factors):
        pivot = spread[j][j : j + 1]
        ratio = jnp.where(row > j, spread[j] / pivot, 0.0)
        for k in range(j + 1, factors):
            spread[k] = spread[k] - ratio * spread[k][j : j + 1]
        inverse = inverse - ratio * inverse[j : j + 1]
        inverse = jnp.where(row == j, inverse / jnp.sqrt(pivot), inverse)
    wide = jnp.concatenate([inverse] * (n // factors), axis=0)
    row = lax.broadcasted_iota(jnp.int32, (n, n), 0) // factors
    lane = lax.broadcasted_iota(jnp.int32, (n, n), 1) // factors
    return jnp.where(row == lane, wide, 0.0)


def signs_kernel(ids_ref, bits_ref, wide_ref, tall_ref):
    reps, clusters = bits_ref.shape
    n, firms = wide_ref.shape
    table = 2.0 * bits_ref[...].astype(jnp.float32) - 1.0
    table = jnp.broadcast_to(table[:, None, :], (reps, n // reps, clusters))
    table = table.reshape(n, clusters).astype(jnp.bfloat16)
    cluster = lax.broadcasted_iota(jnp.int32, (clusters, firms), 0)
    member = jnp.where(cluster == ids_ref[...], 1.0, 0.0).astype(jnp.bfloat16)
    wide = fast(table, member, NN)
    wide_ref[...] = wide
    tall_ref[...] = wide.T


def columns(t, width):
    return (slice(None), slice(t * width, (t + 1) * width))


def rows_of(t, rows):
    return (slice(t * rows, (t + 1) * rows), slice(None))


def bring(pairs, sems):
    copies = [pltpu.make_async_copy(a, b, sems.at[t]) for t, (a, b) in enumerate(pairs)]
    for copy in copies[:AHEAD]:
        copy.start()
    return copies


def arrive(copies, t):
    for p in range(t * PIECES, (t + 1) * PIECES):
        copies[p].wait()
        if p + AHEAD < len(copies):
            copies[p + AHEAD].start()


def piece_pairs(res_any, res_ref, piece):
    size = res_ref.shape[1] if piece is columns else res_ref.shape[0]
    count = STEPS * PIECES
    return [(res_any.at[piece(p, size // count)], res_ref.at[piece(p, size // count)]) for p in range(count)]


def bring_for_core(core, res_any, res_ref, sems):
    days = res_ref.shape[1]
    count = STEPS * PIECES
    width = days // count
    firsts = [pl.multiple_of(((1 - core) if p < count // 2 else core) * (days // 2) + p % (count // 2) * width, width) for p in range(count)]
    pairs = [(res_any.at[:, pl.ds(firsts[p], width)], res_ref.at[columns(p, width)]) for p in range(count)]
    return bring(pairs, sems), firsts[::PIECES]


def first_kernel(
    start_any, factor_any, res_any,
    out_ref,
    start_ref, factor_ref, res_ref, total_ref, sems,
):
    copies, factors, width = out_ref.shape
    firms, days = res_ref.shape
    n = total_ref.shape[1]
    pairs = [(start_any, start_ref), (factor_any, factor_ref)]
    small = [pltpu.make_async_copy(a, b, sems.at[STEPS * PIECES + i]) for i, (a, b) in enumerate(pairs)]
    for copy in small:
        copy.start()
    tiles = [columns(t, days // STEPS) for t in range(STEPS)]
    large = bring(piece_pairs(res_any, res_ref, columns), sems)
    for copy in small:
        copy.wait()
    start = start_ref[...]
    high = start.astype(jnp.bfloat16).astype(jnp.float32)
    both = jnp.concatenate([high, start - high, jnp.zeros((n - 2 * factors, days), jnp.float32)], axis=0)
    both = both.T.astype(jnp.bfloat16)
    mixed = corners(fast(stack(start, "hl"), stack(factor_ref[...], "hl"), NT), factors, factors)
    mixed = jnp.concatenate([mixed, jnp.zeros((factors, width - firms - factors), jnp.float32)], axis=1)
    out_ref[:, :, firms:] = jnp.broadcast_to(mixed[None], (copies, factors, width - firms))
    for t in range(STEPS):
        arrive(large, t)
        high, low = split(res_ref[tiles[t]])
        right = both[t * (days // STEPS) : (t + 1) * (days // STEPS)]
        part = fast(high, right, NN) + fast(low, right, NN)
        total_ref[...] = part if t == 0 else total_ref[...] + part
    total = total_ref[...].T
    total = total[0:factors] + total[factors : 2 * factors]
    out_ref[:, :, 0:firms] = jnp.broadcast_to(total[None], (copies, factors, firms))


def days_from(raw_t, signs_ref, loadings_ref, factor_ref, left_ref, small_ref, right_ref):
    factors = loadings_ref.shape[0]
    n = raw_t.shape[0]
    high, middle, low = split3(raw_t)
    signs = signs_ref[...]
    left_ref[0:n] = (signs * high.astype(jnp.float32)).astype(jnp.bfloat16)
    left_ref[n:] = (signs * middle.astype(jnp.float32)).astype(jnp.bfloat16)
    both = jnp.concatenate([high, middle], axis=0)
    small = corners(fast(stack(loadings_ref[...], "hl"), both, NT), factors, n)
    small_ref[...] = stack(small, "hhl0")
    right_ref[...] = stack(factor_ref[...], "hlh0")
    return compact(gram_of(high, middle, low, NT, 0), factors)


def days_tiles(copies, firsts, res_ref, left_ref, small_ref, right_ref, send_ref, keep_ref):
    n = small_ref.shape[1]
    rows = send_ref.shape[1] - small_ref.shape[0] // 4
    width = res_ref.shape[1] // STEPS
    half = STEPS // 2
    for t in range(STEPS):
        arrive(copies, t)
        high, low = split(res_ref[columns(t, width)])
        both = fast(left_ref[...], high, NN)
        more = fast(small_ref[...], right_ref[:, pl.ds(firsts[t], width)], TN)
        tile = both[0:n] + both[n:] + fast(left_ref[0:n], low, NN) + more
        out_ref = send_ref if t < half else keep_ref
        at = slice(t % half * (width // rows), (t % half + 1) * (width // rows))
        out_ref[at, 0:rows, :] = tile.T.reshape(width // rows, rows, n)


def put_gram(gram, send_ref, keep_ref):
    copies, rows, n = send_ref.shape
    wide = jnp.broadcast_to(gram[None], (copies, gram.shape[0], n))
    send_ref[:, rows - gram.shape[0] :, :] = wide
    keep_ref[:, rows - gram.shape[0] :, :] = wide


def days_first_kernel(core_ref, got_ref, signs_ref, loadings_ref, factor_ref, res_any, send_ref, keep_ref, left_ref, small_ref, right_ref, res_ref, sems):
    copies, firsts = bring_for_core(core_ref[0], res_any, res_ref, sems)
    factors, firms = loadings_ref.shape
    n = signs_ref.shape[0]
    got = got_ref[...].sum(axis=0)
    by_residuals, mixed = got[:, 0:firms], got[:, firms : firms + factors]
    by_factors = jnp.zeros((factors, firms), jnp.float32)
    for m in range(factors):
        by_factors = by_factors + mixed[:, m : m + 1] * loadings_ref[m : m + 1, :]
    reps = n // factors
    raw_t = signs_ref[...] * jnp.concatenate([by_residuals] * reps, axis=0)
    raw_t = raw_t + jnp.concatenate([by_factors] * reps, axis=0)
    put_gram(days_from(raw_t, signs_ref, loadings_ref, factor_ref, left_ref, small_ref, right_ref), send_ref, keep_ref)
    days_tiles(copies, firsts, res_ref, left_ref, small_ref, right_ref, send_ref, keep_ref)


def days_later_kernel(core_ref, got_ref, signs_ref, loadings_ref, factor_ref, res_any, send_ref, keep_ref, left_ref, small_ref, right_ref, res_ref, sems):
    copies, firsts = bring_for_core(core_ref[0], res_any, res_ref, sems)
    put_gram(days_from(got_ref[...].T, signs_ref, loadings_ref, factor_ref, left_ref, small_ref, right_ref), send_ref, keep_ref)
    days_tiles(copies, firsts, res_ref, left_ref, small_ref, right_ref, send_ref, keep_ref)


def firms_kernel(core_ref, mine_ref, other_ref, signs_ref, loadings_ref, factor_ref, res_any, out_ref, raw_ref, right_ref, add_ref, res_ref, sems):
    factors = loadings_ref.shape[0]
    half, n = mine_ref.shape
    rows = res_ref.shape[0] // STEPS
    large = bring(piece_pairs(res_any, res_ref, rows_of), sems)
    core = core_ref[0]
    raw_ref[pl.ds(pl.multiple_of(core * half, half), half), :] = mine_ref[...]
    raw_ref[pl.ds(pl.multiple_of((1 - core) * half, half), half), :] = other_ref[...]
    raw = raw_ref[...]
    high, middle, low = split3(raw)
    right_ref[:, 0:n] = high
    right_ref[:, n:] = middle
    gram = compact(gram_of(high, middle, low, TN, 1), factors)
    copies, total = out_ref.shape[0], out_ref.shape[1]
    out_ref[:, total - factors :, :] = jnp.broadcast_to(gram[None], (copies, factors, n))
    small = corners(fast(stack(factor_ref[...], "hl"), right_ref[...], NN), factors, n)
    add_ref[...] = fast(stack(loadings_ref[...], "hlh0"), stack(small, "hhl0"), TN)
    block = total - factors
    for t in range(STEPS):
        arrive(large, t)
        at = slice(t * rows, (t + 1) * rows)
        high, low = split(res_ref[at, :])
        both = fast(high, right_ref[...], NN)
        part = both[:, 0:n] + both[:, n:] + fast(low, right_ref[:, 0:n], NN)
        part = signs_ref[at, :] * part + add_ref[at, :]
        out_ref[t * rows // block : (t + 1) * rows // block, 0:block, :] = part.reshape(rows // block, block, n)


def turn_kernel(got_ref, out_ref, *inverse_ref):
    copies, rows, _ = out_ref.shape
    total = got_ref[...].sum(axis=0)
    inverse = inverse_blocks(total[rows:], total.shape[0] - rows)
    for ref in inverse_ref:
        ref[...] = inverse
    chunk = exact(total[0:rows], inverse, NT)
    out_ref[...] = jnp.broadcast_to(chunk[None], out_ref.shape)


def last_kernel(mine_ref, other_ref, out_ref):
    mine, other = mine_ref[...], other_ref[...]
    gram = compact(gram_of(*split3(mine), TN, 1) + gram_of(*split3(other), TN, 1), out_ref.shape[1])
    out_ref[...] = jnp.broadcast_to(gram[None], out_ref.shape)


def loadings_kernel(raw_ref, inverse_ref, out_ref, *, scale):
    out_ref[...] = rotated(raw_ref[...], turning(scale * inverse_ref[...]))


def factors_kernel(core_ref, got_ref, mine_ref, other_ref, out_any, buffer_ref, sems, *, scale):
    half = mine_ref.shape[0]
    rows = half // 2
    gram = got_ref[...].sum(axis=0)
    right = turning(scale * inverse_blocks(gram, gram.shape[0]))
    core = core_ref[0]
    copies = []
    for t in range(4):
        ref, side = (mine_ref, core) if t < 2 else (other_ref, 1 - core)
        at = slice(t % 2 * rows, (t % 2 + 1) * rows)
        buffer_ref[t] = rotated(ref[at, :], right)
        to = pl.ds(pl.multiple_of(side * half + t % 2 * rows, rows), rows)
        copies.append(pltpu.make_async_copy(buffer_ref.at[t], out_any.at[to, :], sems.at[t]))
        copies[t].start()
    for copy in copies:
        copy.wait()


def shape(*dims):
    return jax.ShapeDtypeStruct(dims, jnp.float32)


def inputs(count):
    small = [pl.BlockSpec(memory_space=pltpu.VMEM)] * count
    return [pl.BlockSpec(memory_space=pltpu.SMEM), *small]


def in_hbm(x):
    return pltpu.with_memory_space_constraint(x, pltpu.HBM)


def on_device(residuals, loadings, factor_path, start_guess, cluster_ids, sign_bits, *, chips, total_firms, total_days, day_ranks):
    firms, days = residuals.shape
    factors = start_guess.shape[1]
    clusters, reps = sign_bits.shape
    n = reps * factors
    half = days // 2
    chunk = half // chips
    block = firms // day_ranks
    loadings_t, factor_t, start_t = loadings.T, factor_path.T, start_guess.T
    core = lax.axis_index("core").astype(jnp.int32).reshape(1)

    residuals = in_hbm(residuals)
    block_scratch = [pltpu.VMEM((firms, days), jnp.float32), pltpu.SemaphoreType.DMA((STEPS * PIECES,))]
    first = pl.pallas_call(
        first_kernel,
        in_specs=[pl.BlockSpec(memory_space=pl.ANY)] * 3,
        out_shape=shape(day_ranks, factors, firms + n),
        scratch_shapes=[
            pltpu.VMEM((factors, days), jnp.float32),
            pltpu.VMEM((factors, days), jnp.float32),
            pltpu.VMEM((firms, days), jnp.float32),
            pltpu.VMEM((firms, n), jnp.float32),
            pltpu.SemaphoreType.DMA((STEPS * PIECES + 2,)),
        ],
        compiler_params=PARAMS,
        name="first",
    )(in_hbm(start_t), in_hbm(factor_t), residuals)
    signs_t, signs = pl.pallas_call(
        signs_kernel,
        out_shape=(shape(n, firms), shape(firms, n)),
        compiler_params=PARAMS,
        name="signs",
    )(cluster_ids.reshape(1, firms), sign_bits.T)
    first = lax.all_to_all(first, ("x_hi", "y"), 0, 0, tiled=True)

    day_scratch = [
        pltpu.VMEM((2 * n, firms), jnp.bfloat16),
        pltpu.VMEM((4 * factors, n), jnp.bfloat16),
        pltpu.VMEM((4 * factors, days), jnp.bfloat16),
        *block_scratch,
    ]
    any_space = pl.BlockSpec(memory_space=pl.ANY)
    parts = (chips, chunk + factors, n)

    def turn(got, rows, with_inverse):
        out = shape(got.shape[0], rows, n)
        return pl.pallas_call(
            turn_kernel,
            out_shape=(out, shape(n, n)) if with_inverse else out,
            compiler_params=PARAMS,
            name="turn",
        )(got)

    def scatter_firms(send, keep):
        pair = keep + lax.ppermute(send, "core", [(0, 1), (1, 0)])
        return lax.all_to_all(pair, ("x_lo", "z"), 0, 0, tiled=True)

    def gather_firms(mine):
        mine = lax.all_to_all(mine, ("x_lo", "z"), 0, 0, tiled=True).reshape(half, n)
        return mine, lax.ppermute(mine, "core", [(0, 1), (1, 0)])

    send, keep = pl.pallas_call(
        days_first_kernel,
        in_specs=inputs(4) + [pl.BlockSpec(memory_space=pl.ANY)],
        scratch_shapes=day_scratch,
        out_shape=(shape(*parts), shape(*parts)),
        compiler_params=PARAMS,
        name="days_first",
    )(core, first, signs_t, loadings_t, factor_t, residuals)
    mine, other = gather_firms(turn(scatter_firms(send, keep), chunk, False))

    by_day = pl.pallas_call(
        firms_kernel,
        in_specs=inputs(5) + [pl.BlockSpec(memory_space=pl.ANY)],
        scratch_shapes=[
            pltpu.VMEM((days, n), jnp.float32),
            pltpu.VMEM((days, 2 * n), jnp.bfloat16),
            pltpu.VMEM((firms, n), jnp.float32),
            *block_scratch,
        ],
        out_shape=shape(day_ranks, block + factors, n),
        compiler_params=PARAMS,
        name="firms",
    )(core, mine, other, signs, loadings_t, factor_t, residuals)
    raw_loads = turn(lax.all_to_all(by_day, ("x_hi", "y"), 0, 0, tiled=True), block, False)
    raw_loads = lax.all_to_all(raw_loads, ("x_hi", "y"), 0, 0, tiled=True).reshape(firms, n)

    send, keep = pl.pallas_call(
        days_later_kernel,
        in_specs=inputs(4) + [pl.BlockSpec(memory_space=pl.ANY)],
        scratch_shapes=day_scratch,
        out_shape=(shape(*parts), shape(*parts)),
        compiler_params=PARAMS,
        name="days_later",
    )(core, raw_loads, signs_t, loadings_t, factor_t, residuals)
    mine, inverse = turn(scatter_firms(send, keep), chunk, True)
    mine, other = gather_firms(mine)

    last = pl.pallas_call(
        last_kernel,
        out_shape=shape(day_ranks, factors, n),
        compiler_params=PARAMS,
        name="last",
    )(mine, other)
    boot_loadings = pl.pallas_call(
        functools.partial(loadings_kernel, scale=math.sqrt(total_firms)),
        out_shape=shape(firms, n),
        compiler_params=PARAMS,
        name="boot_loadings",
    )(raw_loads, inverse)
    last, boot_loadings = lax.optimization_barrier((last, boot_loadings))
    last = lax.all_to_all(last, ("x_hi", "y"), 0, 0, tiled=True)
    boot_factors = pl.pallas_call(
        functools.partial(factors_kernel, scale=math.sqrt(total_days)),
        in_specs=inputs(3),
        out_specs=any_space,
        out_shape=shape(days, n),
        scratch_shapes=[pltpu.VMEM((4, days // 4, n), jnp.float32), pltpu.SemaphoreType.DMA((4,))],
        compiler_params=PARAMS,
        name="boot_factors",
    )(core, last, mine, other)
    return boot_loadings, boot_factors


def solution(mesh):
    firm_ranks, day_ranks = mesh.shape["firm"], mesh.shape["day"]
    axes = ("x_lo", "z", "core", "x_hi", "y")
    fine = Mesh(mesh.devices.reshape(2, firm_ranks // 4, 2, 2, day_ranks // 2), axes)
    firm, day = ("x_lo", "z", "core"), ("x_hi", "y")

    def run(residuals, *rest):
        total_firms, total_days = residuals.shape
        body = functools.partial(
            on_device, chips=firm_ranks // 2, total_firms=total_firms, total_days=total_days, day_ranks=day_ranks
        )
        return jax.shard_map(
            body,
            mesh=fine,
            in_specs=(P(firm, day), P(firm, None), P(day, None), P(day, None), P(firm), P()),
            out_specs=(P(firm, None), P(day, None)),
            check_vma=False,
        )(residuals, *rest)

    return run
```

```python
import functools
import math

import jax
import jax.numpy as jnp
from jax import lax
from jax.experimental import pallas as pl
from jax.experimental.pallas import tpu as pltpu
from jax.sharding import Mesh
from jax.sharding import PartitionSpec as P

STEPS = 4
PIECES = 2
AHEAD = 8
HIGHEST = lax.Precision.HIGHEST
NN = (((1,), (0,)), ((), ()))
NT = (((1,), (1,)), ((), ()))
TN = (((0,), (0,)), ((), ()))
PARAMS = pltpu.CompilerParams(vmem_limit_bytes=32 * 1024 * 1024)


def exact(a, b, dims):
    return lax.dot_general(a, b, dims, precision=HIGHEST, preferred_element_type=jnp.float32)


def fast(a, b, dims):
    return lax.dot_general(a, b, dims, preferred_element_type=jnp.float32)


def split(x):
    high = x.astype(jnp.bfloat16)
    return high, (x - high.astype(jnp.float32)).astype(jnp.bfloat16)


def split3(x):
    high = x.astype(jnp.bfloat16)
    rest = x - high.astype(jnp.float32)
    middle = rest.astype(jnp.bfloat16)
    return high, middle, (rest - middle.astype(jnp.float32)).astype(jnp.bfloat16)


def corners(both, rows, cols):
    return both[:rows, :cols] + (both[:rows, cols:] + both[rows:, :cols] + both[rows:, cols:])


def gram_of(high, middle, low, dims, axis):
    both = jnp.concatenate([high, middle], axis=axis)
    n = both.shape[axis] // 2
    cross = fast(high, low, dims)
    return corners(fast(both, both, dims), n, n) + (cross + cross.T)


def stack(x, order):
    high = x.astype(jnp.bfloat16).astype(jnp.float32)
    parts = {"h": high, "l": x - high, "0": jnp.zeros_like(x)}
    return jnp.concatenate([parts[p] for p in order], axis=0).astype(jnp.bfloat16)


def turning(inverse):
    top, rest = split(inverse.T)
    return jnp.concatenate(
        [jnp.concatenate([top, rest], axis=1), jnp.concatenate([top, jnp.zeros_like(rest)], axis=1)], axis=0
    )


def rotated(x, right):
    n = x.shape[1]
    both = fast(jnp.concatenate(split(x), axis=1), right, NN)
    return both[:, 0:n] + both[:, n:]


def compact(full, factors):
    n = full.shape[0]
    row = lax.broadcasted_iota(jnp.int32, (n, n), 0) // factors
    lane = lax.broadcasted_iota(jnp.int32, (n, n), 1) // factors
    kept = jnp.where(row == lane, full, 0.0)
    return kept.reshape(n // factors, factors, n).sum(axis=0)


def inverse_blocks(gram, factors):
    n = gram.shape[1]
    row = lax.broadcasted_iota(jnp.int32, (factors, n), 0)
    lane = lax.broadcasted_iota(jnp.int32, (factors, n), 1)
    first = (lane // factors) * factors
    inverse = jnp.where(row == lane - first, 1.0, 0.0)
    spread = [jnp.take_along_axis(gram, first + j, axis=1, mode="promise_in_bounds") for j in range(factors)]
    for j in range(factors):
        pivot = spread[j][j : j + 1]
        ratio = jnp.where(row > j, spread[j] / pivot, 0.0)
        for k in range(j + 1, factors):
            spread[k] = spread[k] - ratio * spread[k][j : j + 1]
        inverse = inverse - ratio * inverse[j : j + 1]
        inverse = jnp.where(row == j, inverse / jnp.sqrt(pivot), inverse)
    wide = jnp.concatenate([inverse] * (n // factors), axis=0)
    row = lax.broadcasted_iota(jnp.int32, (n, n), 0) // factors
    lane = lax.broadcasted_iota(jnp.int32, (n, n), 1) // factors
    return jnp.where(row == lane, wide, 0.0)


def signs_kernel(ids_ref, bits_ref, wide_ref, tall_ref):
    reps, clusters = bits_ref.shape
    n, firms = wide_ref.shape
    table = 2.0 * bits_ref[...].astype(jnp.float32) - 1.0
    table = jnp.broadcast_to(table[:, None, :], (reps, n // reps, clusters))
    table = table.reshape(n, clusters).astype(jnp.bfloat16)
    cluster = lax.broadcasted_iota(jnp.int32, (clusters, firms), 0)
    member = jnp.where(cluster == ids_ref[...], 1.0, 0.0).astype(jnp.bfloat16)
    wide = fast(table, member, NN)
    wide_ref[...] = wide
    tall_ref[...] = wide.T


def columns(t, width):
    return (slice(None), slice(t * width, (t + 1) * width))


def rows_of(t, rows):
    return (slice(t * rows, (t + 1) * rows), slice(None))


def bring(pairs, sems):
    copies = [pltpu.make_async_copy(a, b, sems.at[t]) for t, (a, b) in enumerate(pairs)]
    for copy in copies[:AHEAD]:
        copy.start()
    return copies


def arrive(copies, t):
    for p in range(t * PIECES, (t + 1) * PIECES):
        copies[p].wait()
        if p + AHEAD < len(copies):
            copies[p + AHEAD].start()


def piece_pairs(res_any, res_ref, piece):
    size = res_ref.shape[1] if piece is columns else res_ref.shape[0]
    count = STEPS * PIECES
    return [(res_any.at[piece(p, size // count)], res_ref.at[piece(p, size // count)]) for p in range(count)]


def bring_for_core(core, res_any, res_ref, sems):
    days = res_ref.shape[1]
    count = STEPS * PIECES
    width = days // count
    firsts = [pl.multiple_of(((1 - core) if p < count // 2 else core) * (days // 2) + p % (count // 2) * width, width) for p in range(count)]
    pairs = [(res_any.at[:, pl.ds(firsts[p], width)], res_ref.at[columns(p, width)]) for p in range(count)]
    return bring(pairs, sems), firsts[::PIECES]


def first_kernel(
    start_any, factor_any, res_any,
    out_ref,
    start_ref, factor_ref, res_ref, total_ref, sems,
):
    copies, factors, width = out_ref.shape
    firms, days = res_ref.shape
    n = total_ref.shape[1]
    pairs = [(start_any, start_ref), (factor_any, factor_ref)]
    small = [pltpu.make_async_copy(a, b, sems.at[STEPS * PIECES + i]) for i, (a, b) in enumerate(pairs)]
    for copy in small:
        copy.start()
    tiles = [columns(t, days // STEPS) for t in range(STEPS)]
    large = bring(piece_pairs(res_any, res_ref, columns), sems)
    for copy in small:
        copy.wait()
    start = start_ref[...]
    high = start.astype(jnp.bfloat16).astype(jnp.float32)
    both = jnp.concatenate([high, start - high, jnp.zeros((n - 2 * factors, days), jnp.float32)], axis=0)
    both = both.T.astype(jnp.bfloat16)
    mixed = corners(fast(stack(start, "hl"), stack(factor_ref[...], "hl"), NT), factors, factors)
    mixed = jnp.concatenate([mixed, jnp.zeros((factors, width - firms - factors), jnp.float32)], axis=1)
    out_ref[:, :, firms:] = jnp.broadcast_to(mixed[None], (copies, factors, width - firms))
    for t in range(STEPS):
        arrive(large, t)
        high, low = split(res_ref[tiles[t]])
        right = both[t * (days // STEPS) : (t + 1) * (days // STEPS)]
        part = fast(high, right, NN) + fast(low, right, NN)
        total_ref[...] = part if t == 0 else total_ref[...] + part
    total = total_ref[...].T
    total = total[0:factors] + total[factors : 2 * factors]
    out_ref[:, :, 0:firms] = jnp.broadcast_to(total[None], (copies, factors, firms))


def days_from(raw_t, signs_ref, loadings_ref, factor_ref, left_ref, small_ref, right_ref):
    factors = loadings_ref.shape[0]
    n = raw_t.shape[0]
    high, middle, low = split3(raw_t)
    signs = signs_ref[...]
    left_ref[0:n] = (signs * high.astype(jnp.float32)).astype(jnp.bfloat16)
    left_ref[n:] = (signs * middle.astype(jnp.float32)).astype(jnp.bfloat16)
    both = jnp.concatenate([high, middle], axis=0)
    small = corners(fast(stack(loadings_ref[...], "hl"), both, NT), factors, n)
    small_ref[...] = stack(small, "hhl0")
    right_ref[...] = stack(factor_ref[...], "hlh0")
    return compact(gram_of(high, middle, low, NT, 0), factors)


def days_tiles(copies, firsts, res_ref, left_ref, small_ref, right_ref, send_ref, keep_ref):
    n = small_ref.shape[1]
    rows = send_ref.shape[1] - small_ref.shape[0] // 4
    width = res_ref.shape[1] // STEPS
    half = STEPS // 2
    for t in range(STEPS):
        arrive(copies, t)
        high, low = split(res_ref[columns(t, width)])
        both = fast(left_ref[...], high, NN)
        more = fast(small_ref[...], right_ref[:, pl.ds(firsts[t], width)], TN)
        tile = both[0:n] + both[n:] + fast(left_ref[0:n], low, NN) + more
        out_ref = send_ref if t < half else keep_ref
        at = slice(t % half * (width // rows), (t % half + 1) * (width // rows))
        out_ref[at, 0:rows, :] = tile.T.reshape(width // rows, rows, n)


def put_gram(gram, send_ref, keep_ref):
    copies, rows, n = send_ref.shape
    wide = jnp.broadcast_to(gram[None], (copies, gram.shape[0], n))
    send_ref[:, rows - gram.shape[0] :, :] = wide
    keep_ref[:, rows - gram.shape[0] :, :] = wide


def days_first_kernel(core_ref, got_ref, signs_ref, loadings_ref, factor_ref, res_any, send_ref, keep_ref, left_ref, small_ref, right_ref, res_ref, sems):
    copies, firsts = bring_for_core(core_ref[0], res_any, res_ref, sems)
    factors, firms = loadings_ref.shape
    n = signs_ref.shape[0]
    got = got_ref[...].sum(axis=0)
    by_residuals, mixed = got[:, 0:firms], got[:, firms : firms + factors]
    by_factors = jnp.zeros((factors, firms), jnp.float32)
    for m in range(factors):
        by_factors = by_factors + mixed[:, m : m + 1] * loadings_ref[m : m + 1, :]
    reps = n // factors
    raw_t = signs_ref[...] * jnp.concatenate([by_residuals] * reps, axis=0)
    raw_t = raw_t + jnp.concatenate([by_factors] * reps, axis=0)
    put_gram(days_from(raw_t, signs_ref, loadings_ref, factor_ref, left_ref, small_ref, right_ref), send_ref, keep_ref)
    days_tiles(copies, firsts, res_ref, left_ref, small_ref, right_ref, send_ref, keep_ref)


def days_later_kernel(core_ref, got_ref, signs_ref, loadings_ref, factor_ref, res_any, send_ref, keep_ref, left_ref, small_ref, right_ref, res_ref, sems):
    copies, firsts = bring_for_core(core_ref[0], res_any, res_ref, sems)
    put_gram(days_from(got_ref[...].T, signs_ref, loadings_ref, factor_ref, left_ref, small_ref, right_ref), send_ref, keep_ref)
    days_tiles(copies, firsts, res_ref, left_ref, small_ref, right_ref, send_ref, keep_ref)


def firms_kernel(core_ref, mine_ref, other_ref, signs_ref, loadings_ref, factor_ref, res_any, out_ref, right_ref, add_ref, res_ref, sems):
    factors = loadings_ref.shape[0]
    half, n = mine_ref.shape
    rows = res_ref.shape[0] // STEPS
    large = bring(piece_pairs(res_any, res_ref, rows_of), sems)
    core = core_ref[0]
    gram = jnp.zeros((n, n), jnp.float32)
    for ref, side in ((mine_ref, core), (other_ref, 1 - core)):
        high, middle, low = split3(ref[...])
        at = pl.ds(pl.multiple_of(side * half, half), half)
        right_ref[at, 0:n] = high
        right_ref[at, n:] = middle
        gram = gram + gram_of(high, middle, low, TN, 1)
    gram = compact(gram, factors)
    copies, total = out_ref.shape[0], out_ref.shape[1]
    out_ref[:, total - factors :, :] = jnp.broadcast_to(gram[None], (copies, factors, n))
    small = corners(fast(stack(factor_ref[...], "hl"), right_ref[...], NN), factors, n)
    add_ref[...] = fast(stack(loadings_ref[...], "hlh0"), stack(small, "hhl0"), TN)
    block = total - factors
    for t in range(STEPS):
        arrive(large, t)
        at = slice(t * rows, (t + 1) * rows)
        high, low = split(res_ref[at, :])
        both = fast(high, right_ref[...], NN)
        part = both[:, 0:n] + both[:, n:] + fast(low, right_ref[:, 0:n], NN)
        part = signs_ref[at, :] * part + add_ref[at, :]
        out_ref[t * rows // block : (t + 1) * rows // block, 0:block, :] = part.reshape(rows // block, block, n)


def turn_kernel(got_ref, out_ref, *inverse_ref):
    copies, rows, _ = out_ref.shape
    total = got_ref[...].sum(axis=0)
    inverse = inverse_blocks(total[rows:], total.shape[0] - rows)
    for ref in inverse_ref:
        ref[...] = inverse
    chunk = exact(total[0:rows], inverse, NT)
    out_ref[...] = jnp.broadcast_to(chunk[None], out_ref.shape)


def last_kernel(mine_ref, other_ref, out_ref):
    mine, other = mine_ref[...], other_ref[...]
    gram = compact(gram_of(*split3(mine), TN, 1) + gram_of(*split3(other), TN, 1), out_ref.shape[1])
    out_ref[...] = jnp.broadcast_to(gram[None], out_ref.shape)


def loadings_kernel(raw_ref, inverse_ref, out_ref, *, scale):
    out_ref[...] = rotated(raw_ref[...], turning(scale * inverse_ref[...]))


def factors_kernel(core_ref, got_ref, mine_ref, other_ref, out_any, buffer_ref, sems, *, scale):
    half = mine_ref.shape[0]
    rows = half // 2
    gram = got_ref[...].sum(axis=0)
    right = turning(scale * inverse_blocks(gram, gram.shape[0]))
    core = core_ref[0]
    copies = []
    for t in range(4):
        ref, side = (mine_ref, core) if t < 2 else (other_ref, 1 - core)
        at = slice(t % 2 * rows, (t % 2 + 1) * rows)
        buffer_ref[t] = rotated(ref[at, :], right)
        to = pl.ds(pl.multiple_of(side * half + t % 2 * rows, rows), rows)
        copies.append(pltpu.make_async_copy(buffer_ref.at[t], out_any.at[to, :], sems.at[t]))
        copies[t].start()
    for copy in copies:
        copy.wait()


def shape(*dims):
    return jax.ShapeDtypeStruct(dims, jnp.float32)


def inputs(count):
    small = [pl.BlockSpec(memory_space=pltpu.VMEM)] * count
    return [pl.BlockSpec(memory_space=pltpu.SMEM), *small]


def in_hbm(x):
    return pltpu.with_memory_space_constraint(x, pltpu.HBM)


def on_device(residuals, loadings, factor_path, start_guess, cluster_ids, sign_bits, *, chips, total_firms, total_days, day_ranks):
    firms, days = residuals.shape
    factors = start_guess.shape[1]
    clusters, reps = sign_bits.shape
    n = reps * factors
    half = days // 2
    chunk = half // chips
    block = firms // day_ranks
    loadings_t, factor_t, start_t = loadings.T, factor_path.T, start_guess.T
    core = lax.axis_index("core").astype(jnp.int32).reshape(1)

    residuals = in_hbm(residuals)
    block_scratch = [pltpu.VMEM((firms, days), jnp.float32), pltpu.SemaphoreType.DMA((STEPS * PIECES,))]
    first = pl.pallas_call(
        first_kernel,
        in_specs=[pl.BlockSpec(memory_space=pl.ANY)] * 3,
        out_shape=shape(day_ranks, factors, firms + n),
        scratch_shapes=[
            pltpu.VMEM((factors, days), jnp.float32),
            pltpu.VMEM((factors, days), jnp.float32),
            pltpu.VMEM((firms, days), jnp.float32),
            pltpu.VMEM((firms, n), jnp.float32),
            pltpu.SemaphoreType.DMA((STEPS * PIECES + 2,)),
        ],
        compiler_params=PARAMS,
        name="first",
    )(in_hbm(start_t), in_hbm(factor_t), residuals)
    signs_t, signs = pl.pallas_call(
        signs_kernel,
        out_shape=(shape(n, firms), shape(firms, n)),
        compiler_params=PARAMS,
        name="signs",
    )(cluster_ids.reshape(1, firms), sign_bits.T)
    first = lax.all_to_all(first, ("x_hi", "y"), 0, 0, tiled=True)

    day_scratch = [
        pltpu.VMEM((2 * n, firms), jnp.bfloat16),
        pltpu.VMEM((4 * factors, n), jnp.bfloat16),
        pltpu.VMEM((4 * factors, days), jnp.bfloat16),
        *block_scratch,
    ]
    any_space = pl.BlockSpec(memory_space=pl.ANY)
    parts = (chips, chunk + factors, n)

    def turn(got, rows, with_inverse):
        out = shape(got.shape[0], rows, n)
        return pl.pallas_call(
            turn_kernel,
            out_shape=(out, shape(n, n)) if with_inverse else out,
            compiler_params=PARAMS,
            name="turn",
        )(got)

    def scatter_firms(send, keep):
        pair = keep + lax.ppermute(send, "core", [(0, 1), (1, 0)])
        return lax.all_to_all(pair, ("x_lo", "z"), 0, 0, tiled=True)

    def gather_firms(mine):
        mine = lax.all_to_all(mine, ("x_lo", "z"), 0, 0, tiled=True).reshape(half, n)
        return mine, lax.ppermute(mine, "core", [(0, 1), (1, 0)])

    send, keep = pl.pallas_call(
        days_first_kernel,
        in_specs=inputs(4) + [pl.BlockSpec(memory_space=pl.ANY)],
        scratch_shapes=day_scratch,
        out_shape=(shape(*parts), shape(*parts)),
        compiler_params=PARAMS,
        name="days_first",
    )(core, first, signs_t, loadings_t, factor_t, residuals)
    mine, other = gather_firms(turn(scatter_firms(send, keep), chunk, False))

    by_day = pl.pallas_call(
        firms_kernel,
        in_specs=inputs(5) + [pl.BlockSpec(memory_space=pl.ANY)],
        scratch_shapes=[
            pltpu.VMEM((days, 2 * n), jnp.bfloat16),
            pltpu.VMEM((firms, n), jnp.float32),
            *block_scratch,
        ],
        out_shape=shape(day_ranks, block + factors, n),
        compiler_params=PARAMS,
        name="firms",
    )(core, mine, other, signs, loadings_t, factor_t, residuals)
    raw_loads = turn(lax.all_to_all(by_day, ("x_hi", "y"), 0, 0, tiled=True), block, False)
    raw_loads = lax.all_to_all(raw_loads, ("x_hi", "y"), 0, 0, tiled=True).reshape(firms, n)

    send, keep = pl.pallas_call(
        days_later_kernel,
        in_specs=inputs(4) + [pl.BlockSpec(memory_space=pl.ANY)],
        scratch_shapes=day_scratch,
        out_shape=(shape(*parts), shape(*parts)),
        compiler_params=PARAMS,
        name="days_later",
    )(core, raw_loads, signs_t, loadings_t, factor_t, residuals)
    mine, inverse = turn(scatter_firms(send, keep), chunk, True)
    mine, other = gather_firms(mine)

    last = pl.pallas_call(
        last_kernel,
        out_shape=shape(day_ranks, factors, n),
        compiler_params=PARAMS,
        name="last",
    )(mine, other)
    boot_loadings = pl.pallas_call(
        functools.partial(loadings_kernel, scale=math.sqrt(total_firms)),
        out_shape=shape(firms, n),
        compiler_params=PARAMS,
        name="boot_loadings",
    )(raw_loads, inverse)
    last, boot_loadings = lax.optimization_barrier((last, boot_loadings))
    last = lax.all_to_all(last, ("x_hi", "y"), 0, 0, tiled=True)
    boot_factors = pl.pallas_call(
        functools.partial(factors_kernel, scale=math.sqrt(total_days)),
        in_specs=inputs(3),
        out_specs=any_space,
        out_shape=shape(days, n),
        scratch_shapes=[pltpu.VMEM((4, days // 4, n), jnp.float32), pltpu.SemaphoreType.DMA((4,))],
        compiler_params=PARAMS,
        name="boot_factors",
    )(core, last, mine, other)
    return boot_loadings, boot_factors


def solution(mesh):
    firm_ranks, day_ranks = mesh.shape["firm"], mesh.shape["day"]
    axes = ("x_lo", "z", "core", "x_hi", "y")
    fine = Mesh(mesh.devices.reshape(2, firm_ranks // 4, 2, 2, day_ranks // 2), axes)
    firm, day = ("x_lo", "z", "core"), ("x_hi", "y")

    def run(residuals, *rest):
        total_firms, total_days = residuals.shape
        body = functools.partial(
            on_device, chips=firm_ranks // 2, total_firms=total_firms, total_days=total_days, day_ranks=day_ranks
        )
        return jax.shard_map(
            body,
            mesh=fine,
            in_specs=(P(firm, day), P(firm, None), P(day, None), P(day, None), P(firm), P()),
            out_specs=(P(firm, None), P(day, None)),
            check_vma=False,
        )(residuals, *rest)

    return run
```
